512 devices in a mesh: dp: 64 (over z, y), expert: 8 (over x, core).
Axes of the slice: x: 4, y: 8, z: 8, core: 2. Of those that a mesh axis runs over, the one named last changes fastest.
Arguments:
- router_grads: float32 [8, 7168, 384], P('expert', 'dp'), may hold values from -120 to 120
- latent_grads: float32 [8, 7168, 576], P('expert', 'dp'), may hold values from -120 to 120
- router_moment: float32 [7168, 384], P('dp'), may hold values from -6 to 6
- latent_moment: float32 [7168, 576], P('dp'), may hold values from -6 to 6
Outputs:
- router_moment_out: float32 [7168, 384], P('dp')
- latent_moment_out: float32 [7168, 576], P('dp')
- router_update: float32 [7168, 384], P('dp')
- latent_update: float32 [7168, 576], P('dp')
The draws below stay inside these ranges and needn't reach their ends.
All inputs are finite; a program needn't handle non-finite values.
Results may differ from the reference program's by a relative error of at most 0.012.
The reference program's roundings to bfloat16 on the way (of `scaled`, `gram_low`, `gram_step`, `squared`, `mixture` and `factor`) count: a program that leaves them out, or rounds other values in their place, can miss the bound.
Values may be sent and summed in bfloat16 or wider, within the bound.
No kernel may reach another device: no remote copies, remote signals or barrier semaphores. Data moves between devices by JAX's collectives and lax.ppermute only.
A program may use at most 64 MiB of HBM per device.

```python
import math
import jax
import jax.numpy as jnp
from jax import lax

D = 7168
EXPERTS_ALL = 384
KV_OUT = 576
ITERS = 3
GROUPS = 8


def spread_gradient(key, columns):
    keys = jax.random.split(key, 6)
    noise = jax.random.truncated_normal(keys[0], -4.0, 4.0, (GROUPS, D, columns), jnp.float32)
    patterns = jax.random.uniform(keys[4], (3, D, 1), jnp.float32, -1.7, 1.7)
    mixing = jax.random.uniform(keys[5], (3, 1, columns), jnp.float32, -0.6, 0.6)
    shared = patterns[0] * mixing[0] + patterns[1] * mixing[1] + patterns[2] * mixing[2]
    column_scale = jnp.exp(jax.random.uniform(keys[1], (1, 1, columns), jnp.float32) * math.log(10.0))
    row_scale = jnp.exp(jax.random.uniform(keys[2], (1, D, 1), jnp.float32) * math.log(10.0))
    ramp = jnp.power(3.0, jnp.arange(D, dtype=jnp.float32) / D).reshape(1, D, 1)
    return 0.055 * (noise + shared.reshape(1, D, columns)) * column_scale * row_scale * ramp


def draw_router_grads(key, part):
    key = jax.random.fold_in(key, 11)
    return spread_gradient(key, EXPERTS_ALL)


def draw_latent_grads(key, part):
    key = jax.random.fold_in(key, 23)
    return spread_gradient(key, KV_OUT)


def level_of(stream_key, shape, cuts, smallest, high):
    gain, own = 1.0, jax.random.fold_in(stream_key, 6)
    for dim, blocks in cuts:
        steps = jnp.exp(jax.random.uniform(jax.random.fold_in(own, dim), (blocks,), jnp.float32, smallest / len(cuts), high / len(cuts)))
        gain = gain * jnp.repeat(steps, shape[dim] // blocks).reshape([-1 if axis == dim else 1 for axis in range(len(shape))])
    return gain


def gaussian(own_key, dims, deviation, most, shards=(), kind=jnp.bfloat16):
    result = deviation * jax.random.normal(own_key, dims, jnp.float32)
    if shards:
        result = result * level_of(own_key, dims, shards, -0.22, 0.18)
    return jnp.clip(result, -most, most).astype(kind)


def setup_inputs(seed: int = 0) -> dict:
    key_of = jax.random.split(jax.random.key(seed), 5)
    return {
        "router_grads": draw_router_grads(jax.random.fold_in(key_of[4], 71), 0),
        "latent_grads": draw_latent_grads(jax.random.fold_in(key_of[4], 71), 0),
        "router_moment": gaussian(key_of[2], (D, EXPERTS_ALL), 1.0, 6.0, ((0, 64),), jnp.float32),
        "latent_moment": gaussian(key_of[3], (D, KV_OUT), 1.0, 6.0, ((0, 64),), jnp.float32),
    }


COEF_A = 3.4445
COEF_B = -4.775
COEF_C = 2.0315
BETA = 0.95
EPSILON = 1e-07

def stored(value):
    return lax.optimization_barrier(value.astype(jnp.bfloat16))

def square_dot(left, right):
    return jnp.dot(left, right, preferred_element_type=jnp.float32)

def column_gram(scaled):
    return lax.dot_general(scaled, scaled, (((0,), (0,)), ((), ())), preferred_element_type=jnp.float32)

def apply_factor(scaled, factor):
    product = lax.dot_general(scaled, factor, (((1,), (1,)), ((), ())), preferred_element_type=jnp.float32)
    return product * math.sqrt(D)

def whole_chain(gram_low):
    width = gram_low.shape[0]
    identity = jnp.eye(width, dtype=jnp.float32)
    factor = gram_low
    for iteration in range(ITERS):
        if iteration == 0:
            gram_step = gram_low
        else:
            partial_value = stored(square_dot(factor, gram_low))
            gram_step = stored(square_dot(partial_value, factor))
        squared = stored(square_dot(gram_step, gram_step))
        mixture = stored(COEF_B * gram_step.astype(jnp.float32) + COEF_C * squared.astype(jnp.float32))
        if iteration == 0:
            factor = stored(COEF_A * identity + mixture.astype(jnp.float32))
        else:
            factor = stored(COEF_A * factor.astype(jnp.float32) + square_dot(mixture, factor))
    return factor

def reference(router_grads, latent_grads, router_moment, latent_moment):
    moments_out = []
    updates = []
    for gradient_set, moment in ((router_grads, router_moment), (latent_grads, latent_moment)):
        summed = lax.optimization_barrier(jnp.sum(gradient_set, axis=0))
        moment_new = BETA * moment + summed
        nesterov = summed + BETA * moment_new
        magnitude = jnp.sqrt(jnp.sum(nesterov * nesterov))
        scaled = (nesterov / (magnitude + EPSILON)).astype(jnp.bfloat16)
        factor = whole_chain(stored(column_gram(scaled)))
        moments_out.append(moment_new)
        updates.append(apply_factor(scaled, factor))
    return (moments_out[0], moments_out[1], updates[0], updates[1])
```

```python
import math

import jax
import jax.numpy as jnp
from jax import lax
from jax.sharding import Mesh
from jax.sharding import PartitionSpec as P

D = 7168
ITERS = 3
R = 384
L = 576
T = 128

COEF_A = 3.4445
COEF_B = -4.775
COEF_C = 2.0315
BETA = 0.95
EPSILON = 1e-07
BF = jnp.bfloat16
F32 = jnp.float32


def stored(value):
    return lax.optimization_barrier(value.astype(BF))


def square_dot(left, right):
    return jnp.dot(left, right, preferred_element_type=F32)


def column_gram(value):
    return lax.dot_general(value, value, (((0,), (0,)), ((), ())), preferred_element_type=F32)


def apply_factor(scaled, factor):
    product = lax.dot_general(
        scaled, factor, (((1,), (1,)), ((), ())), preferred_element_type=F32
    )
    return product * math.sqrt(D)


def whole_chain(gram_low):
    width = gram_low.shape[0]
    identity = jnp.eye(width, dtype=F32)
    factor = gram_low
    for iteration in range(ITERS):
        if iteration == 0:
            gram_step = gram_low
        else:
            partial_value = stored(square_dot(factor, gram_low))
            gram_step = stored(square_dot(partial_value, factor))
        squared = stored(square_dot(gram_step, gram_step))
        mixture = stored(COEF_B * gram_step.astype(F32) + COEF_C * squared.astype(F32))
        if iteration == 0:
            factor = stored(COEF_A * identity + mixture.astype(F32))
        else:
            factor = stored(COEF_A * factor.astype(F32) + square_dot(mixture, factor))
    return factor


def split3(value):
    high = lax.reduce_precision(value, 8, 7)
    rest = value - high
    middle = lax.reduce_precision(rest, 8, 7)
    return [high, middle, rest - middle]


def pack(gram_r, gram_l):
    tiles = [
        gram_r[T * i : T * (i + 1), T * j : T * (j + 1)] for i in range(3) for j in range(i, 3)
    ]
    tiles += [
        gram_l[T * i : T * (i + 1), T * j : T * (j + 1)] for i in range(4) for j in range(i, 4)
    ]
    tiles += [gram_l[512:576, T * j : T * (j + 1)] for j in range(4)]
    corner = gram_l[512:576, 512:576]
    tiles.append(jnp.concatenate([corner, jnp.zeros_like(corner)], axis=1))
    tiles.append(jnp.zeros((64, T), corner.dtype))
    return jnp.concatenate(tiles, axis=0)


def unpack(packed):
    at = 0
    whole = []
    for blocks in (3, 4):
        tile = {}
        for i in range(blocks):
            for j in range(i, blocks):
                tile[i, j] = packed[T * at : T * (at + 1)]
                if i != j:
                    tile[j, i] = tile[i, j].T
                at += 1
        whole.append(
            jnp.concatenate(
                [
                    jnp.concatenate([tile[i, j] for j in range(blocks)], axis=1)
                    for i in range(blocks)
                ],
                axis=0,
            )
        )
    base = T * at
    strip = jnp.concatenate([packed[base + 64 * j : base + 64 * (j + 1)] for j in range(4)], axis=1)
    corner = packed[base + 256 : base + 320, :64]
    top = jnp.concatenate([whole[1], strip.T], axis=1)
    bottom = jnp.concatenate([strip, corner], axis=1)
    return whole[0], jnp.concatenate([top, bottom], axis=0)


def local(router_grads, latent_grads, router_moment, latent_moment):
    swap = [(0, 1), (1, 0)]
    router, latent = router_grads[0], latent_grads[0]
    router = router + lax.ppermute(router, "core", swap)
    latent = latent + lax.ppermute(latent, "core", swap)
    chip = stored(jnp.concatenate([router, latent], axis=1))
    parts = lax.all_to_all(jnp.broadcast_to(chip[None], (4,) + chip.shape), "x", 0, 0)
    parts = parts.astype(F32)
    summed = (parts[0] + parts[1]) + (parts[2] + parts[3])

    moments = (router_moment, latent_moment)
    sums = (summed[:, :R], summed[:, R:])
    moment_new = tuple(BETA * moments[k] + sums[k] for k in range(2))
    nesterov = tuple(sums[k] + BETA * moment_new[k] for k in range(2))
    squares = [jnp.sum(nesterov[k] * nesterov[k]) for k in range(2)]
    grams = [column_gram(nesterov[k].astype(BF)) for k in range(2)]
    extra = jnp.stack(split3(squares[0]) + split3(squares[1]))
    extra = jnp.pad(extra, (0, T - 6))
    extra = jnp.broadcast_to(extra[None, None], (64, 2, T))
    packed = pack(grams[0], grams[1]).reshape(64, 38, T)
    payload = stored(jnp.concatenate([packed, extra], axis=1))
    pieces = lax.all_to_all(payload, "dp", 0, 0).astype(F32)
    piece = jnp.sum(pieces, axis=0)
    totals = piece[38]
    squares = [totals[0] + totals[1] + totals[2], totals[3] + totals[4] + totals[5]]
    magnitudes = [jnp.sqrt(square) + EPSILON for square in squares]
    inverse = [1.0 / (magnitude * magnitude) for magnitude in magnitudes]
    row = lax.axis_index("dp") * 38 + lax.iota(jnp.int32, 38)
    scale = jnp.where(row < 6 * T, inverse[0], inverse[1])
    low = stored(piece[:38] * scale[:, None])
    low = jnp.pad(low, ((0, 2), (0, 0)))
    low = lax.all_to_all(jnp.broadcast_to(low[None], (64,) + low.shape), "dp", 0, 0)
    grams_low = unpack(low[:, :38].reshape(19 * T, T))
    updates = []
    for k in range(2):
        scaled = (nesterov[k] / magnitudes[k]).astype(BF)
        updates.append(apply_factor(scaled, whole_chain(stored(grams_low[k]))))
    return (moment_new[0], moment_new[1], updates[0], updates[1])


def solution(mesh):
    inner = Mesh(mesh.devices.reshape(64, 4, 2), ("dp", "x", "core"))
    group = ("x", "core")
    return jax.shard_map(
        local,
        mesh=inner,
        in_specs=(P(group, "dp", None), P(group, "dp", None), P("dp", None), P("dp", None)),
        out_specs=(P("dp", None),) * 4,
        check_vma=False,
    )
```

```python
import functools
import math

import jax
import jax.numpy as jnp
from jax import lax
from jax.experimental import pallas as pl
from jax.experimental.pallas import tpu as pltpu
from jax.sharding import Mesh
from jax.sharding import PartitionSpec as P

D = 7168
ITERS = 3
ROWS = 112
R = 384
L = 576
LP = 640
T = 128
DP = 64
SLABS = 15
PIECE = 16

COEF_A = 3.4445
COEF_B = -4.775
COEF_C = 2.0315
BETA = 0.95
EPSILON = 1e-07
BF = jnp.bfloat16
F32 = jnp.float32

VMEM = pl.BlockSpec(memory_space=pltpu.VMEM)
PARAMS = pltpu.CompilerParams(vmem_limit_bytes=48 * 1024 * 1024)


def dot(left, right):
    return jnp.dot(left, right, preferred_element_type=F32)


def iota(shape, dim):
    return lax.broadcasted_iota(jnp.int32, shape, dim)


def chip_sum_kernel(router, router_other, latent, latent_other, out):
    a = (router[...] + router_other[...]).astype(BF)
    b = (latent[...] + latent_other[...]).astype(BF)
    for copy in range(4):
        out[copy, :, :R] = a
        out[copy, :, R:] = b


def split3(value):
    high = value.astype(BF).astype(F32)
    rest = value - high
    middle = rest.astype(BF).astype(F32)
    return high, middle, rest - middle


def gram_kernel(parts, moment_r, moment_l, new_r, new_l, nest_r, nest_l, payload, slabs, wide):
    core = lax.axis_index("core")
    squares = []
    grams = []
    for first, width, moment, new, nest in (
        (0, R, moment_r, new_r, nest_r),
        (R, L, moment_l, new_l, nest_l),
    ):
        part = [parts[k, :, first : first + width].astype(F32) for k in range(4)]
        summed = (part[0] + part[1]) + (part[2] + part[3])
        fresh = BETA * moment[...] + summed
        nesterov = summed + BETA * fresh
        new[...] = fresh
        nest[...] = nesterov
        squares.append(jnp.sum(nesterov * nesterov))
        low = nesterov.astype(BF)
        if width == L:
            low = jnp.concatenate([low, jnp.zeros((ROWS, LP - L), BF)], axis=1)
        gram = lax.dot_general(low, low, (((0,), (0,)), ((), ())), preferred_element_type=F32)
        grams.append(gram)

    def tile(k, i, j):
        return grams[k][T * i : T * (i + 1), T * j : T * (j + 1)]

    row, lane = iota((T, T), 0), iota((T, T), 1)

    def fold(upper, lower):
        return jnp.where(row <= lane, upper, lower)

    half = iota((64, T), 1) < 64
    last = tile(0, 2, 2)
    corner = jnp.where(half, tile(1, 4, 4)[:64], last[64:])
    tiles = [
        tile(0, 0, 1),
        tile(0, 0, 2),
        tile(0, 1, 2),
        fold(tile(0, 0, 0), tile(0, 1, 1)),
        jnp.concatenate([last[:64], corner], axis=0),
        tile(1, 0, 1),
        tile(1, 0, 2),
        tile(1, 0, 3),
        tile(1, 1, 2),
        tile(1, 1, 3),
        tile(1, 2, 3),
        fold(tile(1, 0, 0), tile(1, 1, 1)),
        fold(tile(1, 2, 2), tile(1, 3, 3)),
    ]
    pieces = [t[64 * h : 64 * (h + 1)] for t in tiles for h in range(2)]
    pieces += [grams[1][512:576, T * j : T * (j + 1)] for j in range(4)]

    parts6 = split3(squares[0]) + split3(squares[1])
    lane1 = iota((64, T), 1)
    row1 = iota((64, T), 0)
    extra = jnp.zeros((64, T), F32)
    for k in range(6):
        extra = jnp.where(lane1 == k, parts6[k], extra)
    for k, (which, i) in enumerate(((0, 1), (1, 1), (1, 3))):
        diagonal = jnp.sum(jnp.where(row == lane, tile(which, i, i), 0.0), axis=0, keepdims=True)
        low_half = pltpu.roll(diagonal, 64, 1)
        extra = jnp.where((row1 == 2 * k) & (lane1 >= 64), low_half, extra)
        extra = jnp.where((row1 == 2 * k + 1) & (lane1 >= 64), diagonal, extra)

    for c in range(2):

        @pl.when(core == c)
        def _():
            for s in range(SLABS):
                slabs[pl.ds(s, DP, stride=PIECE), :] = pieces[SLABS * c + s]

    slabs[pl.ds(SLABS, DP, stride=PIECE), :] = extra
    payload[...] = slabs[...].astype(BF)


def scale_kernel(pieces, low, magnitude):
    core, here = lax.axis_index("core"), lax.axis_index("dp")
    total = jnp.sum(pieces[...].reshape(DP, PIECE, T).astype(F32), axis=0)
    last = total[SLABS : SLABS + 1]
    lane1 = iota((1, T), 1)
    router = jnp.sum(jnp.where(lane1 < 3, last, 0.0), axis=1, keepdims=True)
    latent = jnp.sum(jnp.where((lane1 >= 3) & (lane1 < 6), last, 0.0), axis=1, keepdims=True)
    router = jnp.sqrt(router) + EPSILON
    latent = jnp.sqrt(latent) + EPSILON
    inverse_r = 1.0 / (router * router)
    inverse_l = 1.0 / (latent * latent)
    row, lane = iota((PIECE, T), 0), iota((PIECE, T), 1)
    slab = SLABS * core + row
    of_router = (slab < 9) | ((slab == 9) & (lane >= 64))
    of_router = jnp.where(row == SLABS, jnp.where(here < 2, 1, 0), jnp.where(of_router, 1, 0))
    scaled = (total * jnp.where(of_router == 1, inverse_r, inverse_l)).astype(BF)
    for k in range(DP):
        low[PIECE * k : PIECE * (k + 1), :] = scaled
    magnitude[...] = jnp.where(iota((8, T), 0) == 0, router, latent)


def update_kernel(
    mine, other, magnitude, nest_r, nest_l, out_r, out_l,
    halves, gram_r, gram_l, step_r, step_l, mix_r, mix_l, fac_r, fac_l, tmp_r, tmp_l,
):
    core = lax.axis_index("core")
    a, b = mine[...].astype(F32), other[...].astype(F32)
    first = core == 0
    halves[0] = jnp.where(first, a, b)
    halves[1] = jnp.where(first, b, a)

    def slab(g):
        return halves[g // SLABS, pl.ds(g % SLABS, DP, stride=PIECE), :]

    def tile(t):
        return jnp.concatenate([slab(2 * t), slab(2 * t + 1)], axis=0)

    def put(ref, i, j, value):
        ref[T * i : T * (i + 1), T * j : T * (j + 1)] = value.astype(BF)

    extra = halves[0, pl.ds(SLABS, 8, stride=PIECE), :]
    row, lane = iota((T, T), 0), iota((T, T), 1)
    lane1 = iota((1, T), 1)

    def both(ref, i, j, value):
        put(ref, i, j, value)
        put(ref, j, i, value.T)

    def unfold(ref, i, j, value, k):
        flipped = value.T
        put(ref, i, i, jnp.where(row <= lane, value, flipped))
        low_half = pltpu.roll(extra[2 * k : 2 * k + 1], 64, 1)
        diagonal = jnp.where(lane1 < 64, low_half, extra[2 * k + 1 : 2 * k + 2])
        inner = jnp.where(row > lane, value, flipped)
        put(ref, j, j, jnp.where(row == lane, diagonal, inner))

    both(gram_r, 0, 1, tile(0))
    both(gram_r, 0, 2, tile(1))
    both(gram_r, 1, 2, tile(2))
    unfold(gram_r, 0, 1, tile(3), 0)
    last = tile(4)
    put(gram_r, 2, 2, jnp.where(row <= lane, last, last.T))
    gram_l[L:, :] = jnp.zeros((LP - L, LP), BF)
    gram_l[512:L, 512:] = jnp.where(iota((64, T), 1) < 64, last[64:], 0.0).astype(BF)
    both(gram_l, 0, 1, tile(5))
    both(gram_l, 0, 2, tile(6))
    both(gram_l, 0, 3, tile(7))
    both(gram_l, 1, 2, tile(8))
    both(gram_l, 1, 3, tile(9))
    both(gram_l, 2, 3, tile(10))
    unfold(gram_l, 0, 1, tile(11), 1)
    unfold(gram_l, 2, 3, tile(12), 2)
    for j in range(4):
        strip = jnp.concatenate([slab(26 + j), jnp.zeros((64, T), F32)], axis=0)
        gram_l[512:L, T * j : T * (j + 1)] = strip[:64].astype(BF)
        put(gram_l, j, 4, strip.T)

    for ref in (step_l, mix_l, fac_l, tmp_l):
        ref[L:, :] = jnp.zeros((LP - L, LP), BF)

    def product(left, right, rows, width, epilogue):
        for start in range(0, width, 256):
            stop = min(start + 256, width)
            acc = dot(left[:rows, :], right[:, start:stop])
            epilogue(acc, start, stop)

    def chain(gram, step, mix, fac, tmp, rows, width):
        def store(ref):
            def epilogue(acc, start, stop):
                ref[:rows, start:stop] = acc.astype(BF)

            return epilogue

        for iteration in range(ITERS):
            if iteration == 0:
                now = gram
            else:
                now = step
                product(fac, gram, rows, width, store(tmp))
                yield
                product(tmp, fac, rows, width, store(step))
                yield

            def mixing(acc, start, stop, now=now):
                squared = acc.astype(BF).astype(F32)
                value = COEF_B * now[:rows, start:stop].astype(F32) + COEF_C * squared
                value = value.astype(BF)
                mix[:rows, start:stop] = value
                if iteration == 0:
                    shape = (rows, stop - start)
                    eye = (iota(shape, 0) == iota(shape, 1) + start).astype(F32)
                    fac[:rows, start:stop] = (COEF_A * eye + value.astype(F32)).astype(BF)

            product(now, now, rows, width, mixing)
            yield
            if iteration > 0:

                def blend(acc, start, stop):
                    value = COEF_A * fac[:rows, start:stop].astype(F32) + acc
                    tmp[:rows, start:stop] = value.astype(BF)

                product(mix, fac, rows, width, blend)
                fac, tmp = tmp, fac
                yield
        yield fac

    chains = (
        chain(gram_r, step_r, mix_r, fac_r, tmp_r, R, R),
        chain(gram_l, step_l, mix_l, fac_l, tmp_l, L, LP),
    )
    factors = [None, None]
    for _ in range(4 * ITERS - 2):
        factors = [next(c) for c in chains]
    root = math.sqrt(D)
    contract = (((1,), (1,)), ((), ()))
    scaled = (nest_r[...] / magnitude[0:1, 0:1]).astype(BF)
    out_r[...] = lax.dot_general(scaled, factors[0][...], contract, preferred_element_type=F32) * root
    scaled = (nest_l[...] / magnitude[1:2, 0:1]).astype(BF)
    scaled = jnp.concatenate([scaled, jnp.zeros((ROWS, LP - L), BF)], axis=1)
    out_l[...] = (
        lax.dot_general(scaled, factors[1][:L, :], contract, preferred_element_type=F32) * root
    )


def call(kernel, out_shape, scratch, name, *args):
    return pl.pallas_call(
        kernel,
        out_shape=out_shape,
        in_specs=[VMEM] * len(args),
        out_specs=jax.tree.map(lambda _: VMEM, out_shape),
        scratch_shapes=scratch,
        compiler_params=PARAMS,
        name=name,
    )(*args)


def local(router_grads, latent_grads, router_moment, latent_moment):
    shape = jax.ShapeDtypeStruct
    swap = [(0, 1), (1, 0)]
    router, latent = router_grads[0], latent_grads[0]
    router_other = lax.ppermute(router, "core", swap)
    latent_other = lax.ppermute(latent, "core", swap)
    chip = call(
        chip_sum_kernel, shape((4, ROWS, R + L), BF), [], "chip_sum",
        router, router_other, latent, latent_other,
    )
    parts = lax.all_to_all(chip, "x", 0, 0)
    new_r, new_l, nest_r, nest_l, payload = call(
        gram_kernel,
        (
            shape((ROWS, R), F32), shape((ROWS, L), F32),
            shape((ROWS, R), F32), shape((ROWS, L), F32),
            shape((DP * PIECE, T), BF),
        ),
        [pltpu.VMEM((DP * PIECE, T), F32), pltpu.VMEM((ROWS, LP), BF)],
        "momentum_gram", parts, router_moment, latent_moment,
    )
    pieces = lax.all_to_all(payload.reshape(DP, PIECE, T), "dp", 0, 0)
    low, magnitude = call(
        scale_kernel,
        (shape((DP * PIECE, T), BF), shape((8, T), F32)),
        [], "scale_gram", pieces.reshape(DP * PIECE, T),
    )
    mine = lax.all_to_all(low.reshape(DP, PIECE, T), "dp", 0, 0).reshape(DP * PIECE, T)
    other = lax.ppermute(mine, "core", swap)
    square_r, square_l = pltpu.VMEM((R, R), BF), pltpu.VMEM((LP, LP), BF)
    update_r, update_l = call(
        update_kernel,
        (shape((ROWS, R), F32), shape((ROWS, L), F32)),
        [pltpu.VMEM((2, DP * PIECE, T), F32)] + [square_r, square_l] * 5,
        "chain_apply", mine, other, magnitude, nest_r, nest_l,
    )
    return new_r, new_l, update_r, update_l


def solution(mesh):
    inner = Mesh(mesh.devices.reshape(DP, 4, 2), ("dp", "x", "core"))
    group = ("x", "core")
    return jax.shard_map(
        local,
        mesh=inner,
        in_specs=(P(group, "dp", None), P(group, "dp", None), P("dp", None), P("dp", None)),
        out_specs=(P("dp", None),) * 4,
        check_vma=False,
    )
```

```python
import functools
import math

import jax
import jax.numpy as jnp
from jax import lax
from jax.experimental import pallas as pl
from jax.experimental.pallas import tpu as pltpu
from jax.sharding import Mesh
from jax.sharding import PartitionSpec as P

D = 7168
ITERS = 3
ROWS = 112
R = 384
L = 576
LP = 640
T = 128
DP = 64
SLABS = 15
PIECE = 16

COEF_A = 3.4445
COEF_B = -4.775
COEF_C = 2.0315
BETA = 0.95
EPSILON = 1e-07
BF = jnp.bfloat16
F32 = jnp.float32

VMEM = pl.BlockSpec(memory_space=pltpu.VMEM)
PARAMS = pltpu.CompilerParams(vmem_limit_bytes=48 * 1024 * 1024)


def dot(left, right):
    return jnp.dot(left, right, preferred_element_type=F32)


def iota(shape, dim):
    return lax.broadcasted_iota(jnp.int32, shape, dim)


def chip_sum_kernel(mine, other, out):
    total = (mine[...] + other[...]).astype(BF)
    for copy in range(4):
        out[copy] = total


def split3(value):
    high = value.astype(BF).astype(F32)
    rest = value - high
    middle = rest.astype(BF).astype(F32)
    return high, middle, rest - middle


def gram_kernel(parts, moment_r, moment_l, fresh_r, fresh_l, nest_r, nest_l, payload, slabs):
    core = lax.axis_index("core")
    squares = []
    grams = []
    for first, width, moment, new, nest in (
        (0, R, moment_r, fresh_r, nest_r),
        (R, L, moment_l, fresh_l, nest_l),
    ):
        part = [parts[k, :, first : first + width].astype(F32) for k in range(4)]
        summed = (part[0] + part[1]) + (part[2] + part[3])
        fresh = BETA * moment[...] + summed
        nesterov = summed + BETA * fresh
        new[...] = fresh
        nest[...] = nesterov
        squares.append(jnp.sum(nesterov * nesterov))
        low = nesterov.astype(BF)
        if width == L:
            low = jnp.concatenate([low, jnp.zeros((ROWS, LP - L), BF)], axis=1)
        gram = lax.dot_general(low, low, (((0,), (0,)), ((), ())), preferred_element_type=F32)
        grams.append(gram)

    def tile(k, i, j):
        return grams[k][T * i : T * (i + 1), T * j : T * (j + 1)]

    row, lane = iota((T, T), 0), iota((T, T), 1)

    def fold(upper, lower):
        return jnp.where(row <= lane, upper, lower)

    half = iota((64, T), 1) < 64
    last = tile(0, 2, 2)
    corner = jnp.where(half, tile(1, 4, 4)[:64], last[64:])
    tiles = [
        tile(0, 0, 1),
        tile(0, 0, 2),
        tile(0, 1, 2),
        fold(tile(0, 0, 0), tile(0, 1, 1)),
        jnp.concatenate([last[:64], corner], axis=0),
        tile(1, 0, 1),
        tile(1, 0, 2),
        tile(1, 0, 3),
        tile(1, 1, 2),
        tile(1, 1, 3),
        tile(1, 2, 3),
        fold(tile(1, 0, 0), tile(1, 1, 1)),
        fold(tile(1, 2, 2), tile(1, 3, 3)),
    ]
    pieces = [t[64 * h : 64 * (h + 1)] for t in tiles for h in range(2)]
    pieces += [grams[1][512:576, T * j : T * (j + 1)] for j in range(4)]

    parts6 = split3(squares[0]) + split3(squares[1])
    lane1 = iota((64, T), 1)
    row1 = iota((64, T), 0)
    extra = jnp.zeros((64, T), F32)
    for k in range(6):
        extra = jnp.where(lane1 == k, parts6[k], extra)
    for k, (which, i) in enumerate(((0, 1), (1, 1), (1, 3))):
        diagonal = jnp.sum(jnp.where(row == lane, tile(which, i, i), 0.0), axis=0, keepdims=True)
        low_half = pltpu.roll(diagonal, 64, 1)
        extra = jnp.where((row1 == 2 * k) & (lane1 >= 64), low_half, extra)
        extra = jnp.where((row1 == 2 * k + 1) & (lane1 >= 64), diagonal, extra)

    for c in range(2):

        @pl.when(core == c)
        def _():
            for s in range(SLABS):
                slabs[pl.ds(s, DP, stride=PIECE), :] = pieces[SLABS * c + s]

    slabs[pl.ds(SLABS, DP, stride=PIECE), :] = extra
    payload[...] = slabs[...].astype(BF)


def scale_kernel(pieces, low, magnitude):
    core, here = lax.axis_index("core"), lax.axis_index("dp")
    total = jnp.sum(pieces[...].reshape(DP, PIECE, T).astype(F32), axis=0)
    last = total[SLABS : SLABS + 1]
    lane1 = iota((1, T), 1)
    router = jnp.sum(jnp.where(lane1 < 3, last, 0.0), axis=1, keepdims=True)
    latent = jnp.sum(jnp.where((lane1 >= 3) & (lane1 < 6), last, 0.0), axis=1, keepdims=True)
    router = jnp.sqrt(router) + EPSILON
    latent = jnp.sqrt(latent) + EPSILON
    inverse_r = 1.0 / (router * router)
    inverse_l = 1.0 / (latent * latent)
    row, lane = iota((PIECE, T), 0), iota((PIECE, T), 1)
    slab = SLABS * core + row
    of_router = (slab < 9) | ((slab == 9) & (lane >= 64))
    of_router = jnp.where(row == SLABS, jnp.where(here < 2, 1, 0), jnp.where(of_router, 1, 0))
    scaled = (total * jnp.where(of_router == 1, inverse_r, inverse_l)).astype(BF)
    for k in range(DP):
        low[PIECE * k : PIECE * (k + 1), :] = scaled
    magnitude[...] = jnp.where(iota((8, T), 0) == 0, router, latent)


def update_kernel(
    mine, other, magnitude, nest_r, nest_l, fresh_r, fresh_l, new_r, new_l, out_r, out_l,
    halves, gram_r, gram_l, step_r, step_l, mix_r, mix_l, fac_r, fac_l, tmp_r, tmp_l,
    value_r, value_l, sems,
):
    copies = []

    def write(source, target):
        copies.append(pltpu.make_async_copy(source, target, sems.at[len(copies)]))
        copies[-1].start()

    write(fresh_r, new_r)
    write(fresh_l, new_l)
    core = lax.axis_index("core")
    a, b = mine[...].astype(F32), other[...].astype(F32)
    first = core == 0
    halves[0] = jnp.where(first, a, b)
    halves[1] = jnp.where(first, b, a)

    def slab(g):
        return halves[g // SLABS, pl.ds(g % SLABS, DP, stride=PIECE), :]

    def tile(t):
        return jnp.concatenate([slab(2 * t), slab(2 * t + 1)], axis=0)

    def put(ref, i, j, value):
        ref[T * i : T * (i + 1), T * j : T * (j + 1)] = value.astype(BF)

    extra = halves[0, pl.ds(SLABS, 8, stride=PIECE), :]
    row, lane = iota((T, T), 0), iota((T, T), 1)
    lane1 = iota((1, T), 1)

    def both(ref, i, j, value):
        put(ref, i, j, value)
        put(ref, j, i, value.T)

    def unfold(ref, i, j, value, k):
        flipped = value.T
        put(ref, i, i, jnp.where(row <= lane, value, flipped))
        low_half = pltpu.roll(extra[2 * k : 2 * k + 1], 64, 1)
        diagonal = jnp.where(lane1 < 64, low_half, extra[2 * k + 1 : 2 * k + 2])
        inner = jnp.where(row > lane, value, flipped)
        put(ref, j, j, jnp.where(row == lane, diagonal, inner))

    both(gram_r, 0, 1, tile(0))
    both(gram_r, 0, 2, tile(1))
    both(gram_r, 1, 2, tile(2))
    unfold(gram_r, 0, 1, tile(3), 0)
    last = tile(4)
    put(gram_r, 2, 2, jnp.where(row <= lane, last, last.T))
    gram_l[L:, :] = jnp.zeros((LP - L, LP), BF)
    gram_l[512:L, 512:] = jnp.where(iota((64, T), 1) < 64, last[64:], 0.0).astype(BF)
    both(gram_l, 0, 1, tile(5))
    both(gram_l, 0, 2, tile(6))
    both(gram_l, 0, 3, tile(7))
    both(gram_l, 1, 2, tile(8))
    both(gram_l, 1, 3, tile(9))
    both(gram_l, 2, 3, tile(10))
    unfold(gram_l, 0, 1, tile(11), 1)
    unfold(gram_l, 2, 3, tile(12), 2)
    for j in range(4):
        strip = jnp.concatenate([slab(26 + j), jnp.zeros((64, T), F32)], axis=0)
        gram_l[512:L, T * j : T * (j + 1)] = strip[:64].astype(BF)
        put(gram_l, j, 4, strip.T)

    for ref in (step_l, mix_l, fac_l, tmp_l):
        ref[L:, :] = jnp.zeros((LP - L, LP), BF)

    def product(left, right, rows, width, epilogue):
        for start in range(0, width, 256):
            stop = min(start + 256, width)
            acc = dot(left[:rows, :], right[:, start:stop])
            for ref, value in epilogue(acc, 0, start, stop):
                ref[:rows, start:stop] = value

    def square(gram, rows, width, epilogue):
        edge = (rows - 1) // 256 * 256
        for start in range(0, edge, 256):
            stop = start + 256
            acc = dot(gram[:rows, :], gram[:, start:stop])
            for ref, value in epilogue(acc, 0, start, stop):
                ref[:rows, start:stop] = value
                strip = value[edge:rows].astype(F32)
                if rows - edge < T:
                    strip = jnp.concatenate([strip, jnp.zeros((T + edge - rows, 256), F32)], axis=0)
                ref[start:stop, edge:width] = strip.T.astype(BF)
        acc = dot(gram[edge:rows, :], gram[:, edge:width])
        for ref, value in epilogue(acc, edge, edge, width):
            ref[edge:rows, edge:width] = value

    def chain(gram, step, mix, fac, tmp, rows, width):
        def store(ref):
            return lambda acc, top, start, stop: [(ref, acc.astype(BF))]

        def mixture(now, acc, top, start, stop):
            squared = acc.astype(BF).astype(F32)
            value = COEF_B * now[top : top + acc.shape[0], start:stop].astype(F32) + COEF_C * squared
            return value.astype(BF)

        def begin(acc, top, start, stop):
            value = mixture(gram, acc, top, start, stop)
            eye = (iota(acc.shape, 0) + top == iota(acc.shape, 1) + start).astype(F32)
            return [(fac, (COEF_A * eye + value.astype(F32)).astype(BF))]

        square(gram, rows, width, begin)
        yield
        for _ in range(ITERS - 1):

            def mixing(acc, top, start, stop):
                return [(mix, mixture(step, acc, top, start, stop))]

            def blend(acc, top, start, stop, fac=fac, tmp=tmp):
                value = COEF_A * fac[:rows, start:stop].astype(F32) + acc
                return [(tmp, value.astype(BF))]

            product(fac, gram, rows, width, store(tmp))
            yield
            product(tmp, fac, rows, width, store(step))
            yield
            product(step, step, rows, width, mixing)
            yield
            product(mix, fac, rows, width, blend)
            fac, tmp = tmp, fac
            yield
        yield fac

    root = math.sqrt(D)
    contract = (((1,), (1,)), ((), ()))

    def apply(nest, magnitude, factor, rows, width, value, out):
        scaled = (nest[...] / magnitude).astype(BF)
        if width > rows:
            scaled = jnp.concatenate([scaled, jnp.zeros((ROWS, width - rows), BF)], axis=1)
        for start in range(0, rows, 256):
            stop = min(start + 256, rows)
            part = lax.dot_general(
                scaled, factor[start:stop, :], contract, preferred_element_type=F32
            )
            value[:, start:stop] = part * root
            write(value.at[:, start:stop], out.at[:, start:stop])

    chains = (
        chain(gram_r, step_r, mix_r, fac_r, tmp_r, R, R),
        chain(gram_l, step_l, mix_l, fac_l, tmp_l, L, LP),
    )
    for _ in range(4 * ITERS - 2):
        factors = [next(c) for c in chains]
    apply(nest_r, magnitude[0:1, 0:1], factors[0], R, R, value_r, out_r)
    apply(nest_l, magnitude[1:2, 0:1], factors[1], L, LP, value_l, out_l)
    for copy in copies:
        copy.wait()


def call(kernel, out_shape, scratch, name, *args):
    return pl.pallas_call(
        kernel,
        out_shape=out_shape,
        in_specs=[VMEM] * len(args),
        out_specs=jax.tree.map(lambda _: VMEM, out_shape),
        scratch_shapes=scratch,
        compiler_params=PARAMS,
        name=name,
    )(*args)


def chain_call(mine, other, magnitude, nest_r, nest_l, fresh_r, fresh_l):
    shape = jax.ShapeDtypeStruct
    outs = (shape((ROWS, R), F32), shape((ROWS, L), F32)) * 2
    square_r, square_l = pltpu.VMEM((R, R), BF), pltpu.VMEM((LP, LP), BF)
    return pl.pallas_call(
        update_kernel,
        out_shape=outs,
        in_specs=[VMEM] * 7,
        out_specs=[pl.BlockSpec(memory_space=pl.ANY)] * 4,
        scratch_shapes=[pltpu.VMEM((2, DP * PIECE, T), F32)]
        + [square_r, square_l] * 5
        + [pltpu.VMEM((ROWS, R), F32), pltpu.VMEM((ROWS, L), F32)]
        + [pltpu.SemaphoreType.DMA((7,))],
        compiler_params=PARAMS,
        name="chain_apply",
    )(mine, other, magnitude, nest_r, nest_l, fresh_r, fresh_l)


def local(router_grads, latent_grads, router_moment, latent_moment):
    shape = jax.ShapeDtypeStruct
    swap = [(0, 1), (1, 0)]
    grads = lax.optimization_barrier(jnp.concatenate([router_grads[0], latent_grads[0]], axis=1))
    other = lax.ppermute(grads, "core", swap)
    chip = call(chip_sum_kernel, shape((4, ROWS, R + L), BF), [], "chip_sum", grads, other)
    parts = lax.all_to_all(chip, "x", 0, 0)
    fresh_r, fresh_l, nest_r, nest_l, payload = call(
        gram_kernel,
        (
            shape((ROWS, R), F32), shape((ROWS, L), F32),
            shape((ROWS, R), F32), shape((ROWS, L), F32),
            shape((DP * PIECE, T), BF),
        ),
        [pltpu.VMEM((DP * PIECE, T), F32)], "momentum_gram", parts, router_moment, latent_moment,
    )
    pieces = lax.all_to_all(payload.reshape(DP, PIECE, T), "dp", 0, 0)
    low, magnitude = call(
        scale_kernel,
        (shape((DP * PIECE, T), BF), shape((8, T), F32)),
        [], "scale_gram", pieces.reshape(DP * PIECE, T),
    )
    mine = lax.all_to_all(low.reshape(DP, PIECE, T), "dp", 0, 0).reshape(DP * PIECE, T)
    other = lax.ppermute(mine, "core", swap)
    return chain_call(mine, other, magnitude, nest_r, nest_l, fresh_r, fresh_l)


def solution(mesh):
    inner = Mesh(mesh.devices.reshape(DP, 4, 2), ("dp", "x", "core"))
    group = ("x", "core")
    return jax.shard_map(
        local,
        mesh=inner,
        in_specs=(P(group, "dp", None), P(group, "dp", None), P("dp", None), P("dp", None)),
        out_specs=(P("dp", None),) * 4,
        check_vma=False,
    )
```

```python
import functools
import math

import jax
import jax.numpy as jnp
from jax import lax
from jax.experimental import pallas as pl
from jax.experimental.pallas import tpu as pltpu
from jax.sharding import Mesh
from jax.sharding import PartitionSpec as P

D = 7168
ITERS = 3
ROWS = 112
R = 384
L = 576
LP = 640
T = 128
DP = 64
SLABS = 15
PIECE = 16

COEF_A = 3.4445
COEF_B = -4.775
COEF_C = 2.0315
BETA = 0.95
EPSILON = 1e-07
BF = jnp.bfloat16
F32 = jnp.float32

VMEM = pl.BlockSpec(memory_space=pltpu.VMEM)
PARAMS = pltpu.CompilerParams(vmem_limit_bytes=48 * 1024 * 1024)


def dot(left, right):
    return jnp.dot(left, right, preferred_element_type=F32)


def iota(shape, dim):
    return lax.broadcasted_iota(jnp.int32, shape, dim)


def chip_sum_kernel(mine, other, out):
    total = (mine[...] + other[...]).astype(BF)
    for copy in range(4):
        out[copy] = total


def split3(value):
    high = value.astype(BF).astype(F32)
    rest = value - high
    middle = rest.astype(BF).astype(F32)
    return high, middle, rest - middle


def gram_kernel(parts, moment_r, moment_l, fresh_r, fresh_l, nest_r, nest_l, payload, slabs):
    core = lax.axis_index("core")
    squares = []
    grams = []
    for first, width, moment, new, nest in (
        (0, R, moment_r, fresh_r, nest_r),
        (R, L, moment_l, fresh_l, nest_l),
    ):
        part = [parts[k, :, first : first + width].astype(F32) for k in range(4)]
        summed = (part[0] + part[1]) + (part[2] + part[3])
        fresh = BETA * moment[...] + summed
        nesterov = summed + BETA * fresh
        new[...] = fresh
        nest[...] = nesterov
        squares.append(jnp.sum(nesterov * nesterov))
        low = nesterov.astype(BF)
        if width == L:
            low = jnp.concatenate([low, jnp.zeros((ROWS, LP - L), BF)], axis=1)
        gram = lax.dot_general(low, low, (((0,), (0,)), ((), ())), preferred_element_type=F32)
        grams.append(gram)

    def tile(k, i, j):
        return grams[k][T * i : T * (i + 1), T * j : T * (j + 1)]

    row, lane = iota((T, T), 0), iota((T, T), 1)

    def fold(upper, lower):
        return jnp.where(row <= lane, upper, lower)

    half = iota((64, T), 1) < 64
    last = tile(0, 2, 2)
    corner = jnp.where(half, tile(1, 4, 4)[:64], last[64:])
    tiles = [
        tile(0, 0, 1),
        tile(0, 0, 2),
        tile(0, 1, 2),
        fold(tile(0, 0, 0), tile(0, 1, 1)),
        jnp.concatenate([last[:64], corner], axis=0),
        tile(1, 0, 1),
        tile(1, 0, 2),
        tile(1, 0, 3),
        tile(1, 1, 2),
        tile(1, 1, 3),
        tile(1, 2, 3),
        fold(tile(1, 0, 0), tile(1, 1, 1)),
        fold(tile(1, 2, 2), tile(1, 3, 3)),
    ]
    pieces = [t[64 * h : 64 * (h + 1)] for t in tiles for h in range(2)]
    pieces += [grams[1][512:576, T * j : T * (j + 1)] for j in range(4)]

    parts6 = split3(squares[0]) + split3(squares[1])
    lane1 = iota((64, T), 1)
    row1 = iota((64, T), 0)
    extra = jnp.zeros((64, T), F32)
    for k in range(6):
        extra = jnp.where(lane1 == k, parts6[k], extra)
    for k, (which, i) in enumerate(((0, 1), (1, 1), (1, 3))):
        diagonal = jnp.sum(jnp.where(row == lane, tile(which, i, i), 0.0), axis=0, keepdims=True)
        low_half = pltpu.roll(diagonal, 64, 1)
        extra = jnp.where((row1 == 2 * k) & (lane1 >= 64), low_half, extra)
        extra = jnp.where((row1 == 2 * k + 1) & (lane1 >= 64), diagonal, extra)

    for c in range(2):

        @pl.when(core == c)
        def _():
            for s in range(SLABS):
                slabs[pl.ds(s, DP, stride=PIECE), :] = pieces[SLABS * c + s]

    slabs[pl.ds(SLABS, DP, stride=PIECE), :] = extra
    payload[...] = slabs[...].astype(BF)


def scale_kernel(pieces, low, magnitude):
    core, here = lax.axis_index("core"), lax.axis_index("dp")
    total = jnp.sum(pieces[...].reshape(DP, PIECE, T).astype(F32), axis=0)
    last = total[SLABS : SLABS + 1]
    lane1 = iota((1, T), 1)
    router = jnp.sum(jnp.where(lane1 < 3, last, 0.0), axis=1, keepdims=True)
    latent = jnp.sum(jnp.where((lane1 >= 3) & (lane1 < 6), last, 0.0), axis=1, keepdims=True)
    router = jnp.sqrt(router) + EPSILON
    latent = jnp.sqrt(latent) + EPSILON
    inverse_r = 1.0 / (router * router)
    inverse_l = 1.0 / (latent * latent)
    row, lane = iota((PIECE, T), 0), iota((PIECE, T), 1)
    slab = SLABS * core + row
    of_router = (slab < 9) | ((slab == 9) & (lane >= 64))
    of_router = jnp.where(row == SLABS, jnp.where(here < 2, 1, 0), jnp.where(of_router, 1, 0))
    scaled = (total * jnp.where(of_router == 1, inverse_r, inverse_l)).astype(BF)
    for k in range(DP):
        low[PIECE * k : PIECE * (k + 1), :] = scaled
    magnitude[...] = jnp.where(iota((8, T), 0) == 0, router, latent)


def update_kernel(
    mine, other, magnitude, nest_r, nest_l, fresh_r, fresh_l, new_r, new_l, out_r, out_l,
    halves, gram_r, gram_l, step_r, step_l, mix_r, mix_l, fac_r, fac_l, tmp_r, tmp_l,
    value_r, value_l, sems,
):
    copies = []

    def write(source, target):
        copies.append(pltpu.make_async_copy(source, target, sems.at[len(copies)]))
        copies[-1].start()

    write(fresh_r, new_r)
    write(fresh_l, new_l)
    core = lax.axis_index("core")
    a, b = mine[...].astype(F32), other[...].astype(F32)
    first = core == 0
    halves[0] = jnp.where(first, a, b)
    halves[1] = jnp.where(first, b, a)

    def slab(g):
        return halves[g // SLABS, pl.ds(g % SLABS, DP, stride=PIECE), :]

    def tile(t):
        return jnp.concatenate([slab(2 * t), slab(2 * t + 1)], axis=0)

    def put(ref, i, j, value):
        ref[T * i : T * (i + 1), T * j : T * (j + 1)] = value.astype(BF)

    extra = halves[0, pl.ds(SLABS, 8, stride=PIECE), :]
    row, lane = iota((T, T), 0), iota((T, T), 1)
    lane1 = iota((1, T), 1)

    def both(ref, i, j, value):
        put(ref, i, j, value)
        put(ref, j, i, value.T)

    def unfold(ref, i, j, value, k):
        flipped = value.T
        put(ref, i, i, jnp.where(row <= lane, value, flipped))
        low_half = pltpu.roll(extra[2 * k : 2 * k + 1], 64, 1)
        diagonal = jnp.where(lane1 < 64, low_half, extra[2 * k + 1 : 2 * k + 2])
        inner = jnp.where(row > lane, value, flipped)
        put(ref, j, j, jnp.where(row == lane, diagonal, inner))

    both(gram_r, 0, 1, tile(0))
    both(gram_r, 0, 2, tile(1))
    both(gram_r, 1, 2, tile(2))
    unfold(gram_r, 0, 1, tile(3), 0)
    last = tile(4)
    put(gram_r, 2, 2, jnp.where(row <= lane, last, last.T))
    gram_l[L:, :] = jnp.zeros((LP - L, LP), BF)
    gram_l[512:L, 512:] = jnp.where(iota((64, T), 1) < 64, last[64:], 0.0).astype(BF)
    both(gram_l, 0, 1, tile(5))
    both(gram_l, 0, 2, tile(6))
    both(gram_l, 0, 3, tile(7))
    both(gram_l, 1, 2, tile(8))
    both(gram_l, 1, 3, tile(9))
    both(gram_l, 2, 3, tile(10))
    unfold(gram_l, 0, 1, tile(11), 1)
    unfold(gram_l, 2, 3, tile(12), 2)
    for j in range(4):
        strip = jnp.concatenate([slab(26 + j), jnp.zeros((64, T), F32)], axis=0)
        gram_l[512:L, T * j : T * (j + 1)] = strip[:64].astype(BF)
        put(gram_l, j, 4, strip.T)

    for ref in (step_l, mix_l, fac_l, tmp_l):
        ref[L:, :] = jnp.zeros((LP - L, LP), BF)

    def product(left, right, rows, width, epilogue, symmetric=False):
        if symmetric:
            return mirrored(left, right, rows, width, epilogue)
        for start in range(0, width, 256):
            stop = min(start + 256, width)
            acc = dot(left[:rows, :], right[:, start:stop])
            for ref, value in epilogue(acc, 0, start, stop):
                ref[:rows, start:stop] = value

    def mirrored(left, right, rows, width, epilogue):
        edge = (rows - 1) // 256 * 256
        for start in range(0, edge, 256):
            stop = start + 256
            acc = dot(left[:rows, :], right[:, start:stop])
            for ref, value in epilogue(acc, 0, start, stop):
                ref[:rows, start:stop] = value
                strip = value[edge:rows].astype(F32)
                if rows - edge < T:
                    strip = jnp.concatenate([strip, jnp.zeros((T + edge - rows, 256), F32)], axis=0)
                ref[start:stop, edge:width] = strip.T.astype(BF)
        acc = dot(left[edge:rows, :], right[:, edge:width])
        for ref, value in epilogue(acc, edge, edge, width):
            ref[edge:rows, edge:width] = value

    def chain(gram, step, mix, fac, tmp, rows, width, mirror):
        def store(ref):
            return lambda acc, top, start, stop: [(ref, acc.astype(BF))]

        def mixture(now, acc, top, start, stop):
            squared = acc.astype(BF).astype(F32)
            value = COEF_B * now[top : top + acc.shape[0], start:stop].astype(F32) + COEF_C * squared
            return value.astype(BF)

        def begin(acc, top, start, stop):
            value = mixture(gram, acc, top, start, stop)
            eye = (iota(acc.shape, 0) + top == iota(acc.shape, 1) + start).astype(F32)
            return [(fac, (COEF_A * eye + value.astype(F32)).astype(BF))]

        mirrored(gram, gram, rows, width, begin)
        yield
        for it in range(ITERS - 1):

            def mixing(acc, top, start, stop):
                return [(mix, mixture(step, acc, top, start, stop))]

            def blend(acc, top, start, stop, fac=fac, tmp=tmp):
                value = COEF_A * fac[top : top + acc.shape[0], start:stop].astype(F32) + acc
                return [(tmp, value.astype(BF))]

            product(fac, gram, rows, width, store(tmp), mirror and it == 0)
            yield
            product(tmp, fac, rows, width, store(step), mirror)
            yield
            product(step, step, rows, width, mixing, mirror)
            yield
            product(mix, fac, rows, width, blend, mirror)
            fac, tmp = tmp, fac
            yield
        yield fac

    root = math.sqrt(D)
    contract = (((1,), (1,)), ((), ()))

    def apply(nest, magnitude, factor, rows, width, value, out):
        scaled = (nest[...] / magnitude).astype(BF)
        if width > rows:
            scaled = jnp.concatenate([scaled, jnp.zeros((ROWS, width - rows), BF)], axis=1)
        for start in range(0, rows, 256):
            stop = min(start + 256, rows)
            part = lax.dot_general(
                scaled, factor[start:stop, :], contract, preferred_element_type=F32
            )
            value[:, start:stop] = part * root
            write(value.at[:, start:stop], out.at[:, start:stop])

    chains = (
        chain(gram_r, step_r, mix_r, fac_r, tmp_r, R, R, False),
        chain(gram_l, step_l, mix_l, fac_l, tmp_l, L, LP, True),
    )
    for _ in range(4 * ITERS - 2):
        factors = [next(c) for c in chains]
    apply(nest_r, magnitude[0:1, 0:1], factors[0], R, R, value_r, out_r)
    apply(nest_l, magnitude[1:2, 0:1], factors[1], L, LP, value_l, out_l)
    for copy in copies:
        copy.wait()


def call(kernel, out_shape, scratch, name, *args):
    return pl.pallas_call(
        kernel,
        out_shape=out_shape,
        in_specs=[VMEM] * len(args),
        out_specs=jax.tree.map(lambda _: VMEM, out_shape),
        scratch_shapes=scratch,
        compiler_params=PARAMS,
        name=name,
    )(*args)


def chain_call(mine, other, magnitude, nest_r, nest_l, fresh_r, fresh_l):
    shape = jax.ShapeDtypeStruct
    outs = (shape((ROWS, R), F32), shape((ROWS, L), F32)) * 2
    square_r, square_l = pltpu.VMEM((R, R), BF), pltpu.VMEM((LP, LP), BF)
    return pl.pallas_call(
        update_kernel,
        out_shape=outs,
        in_specs=[VMEM] * 7,
        out_specs=[pl.BlockSpec(memory_space=pl.ANY)] * 4,
        scratch_shapes=[pltpu.VMEM((2, DP * PIECE, T), F32)]
        + [square_r, square_l] * 5
        + [pltpu.VMEM((ROWS, R), F32), pltpu.VMEM((ROWS, L), F32)]
        + [pltpu.SemaphoreType.DMA((7,))],
        compiler_params=PARAMS,
        name="chain_apply",
    )(mine, other, magnitude, nest_r, nest_l, fresh_r, fresh_l)


def local(router_grads, latent_grads, router_moment, latent_moment):
    shape = jax.ShapeDtypeStruct
    swap = [(0, 1), (1, 0)]
    grads = lax.optimization_barrier(jnp.concatenate([router_grads[0], latent_grads[0]], axis=1))
    other = lax.ppermute(grads, "core", swap)
    chip = call(chip_sum_kernel, shape((4, ROWS, R + L), BF), [], "chip_sum", grads, other)
    parts = lax.all_to_all(chip, "x", 0, 0)
    fresh_r, fresh_l, nest_r, nest_l, payload = call(
        gram_kernel,
        (
            shape((ROWS, R), F32), shape((ROWS, L), F32),
            shape((ROWS, R), F32), shape((ROWS, L), F32),
            shape((DP * PIECE, T), BF),
        ),
        [pltpu.VMEM((DP * PIECE, T), F32)], "momentum_gram", parts, router_moment, latent_moment,
    )
    pieces = lax.all_to_all(payload.reshape(DP, PIECE, T), "dp", 0, 0)
    low, magnitude = call(
        scale_kernel,
        (shape((DP * PIECE, T), BF), shape((8, T), F32)),
        [], "scale_gram", pieces.reshape(DP * PIECE, T),
    )
    mine = lax.all_to_all(low.reshape(DP, PIECE, T), "dp", 0, 0).reshape(DP * PIECE, T)
    other = lax.ppermute(mine, "core", swap)
    return chain_call(mine, other, magnitude, nest_r, nest_l, fresh_r, fresh_l)


def solution(mesh):
    inner = Mesh(mesh.devices.reshape(DP, 4, 2), ("dp", "x", "core"))
    group = ("x", "core")
    return jax.shard_map(
        local,
        mesh=inner,
        in_specs=(P(group, "dp", None), P(group, "dp", None), P("dp", None), P("dp", None)),
        out_specs=(P("dp", None),) * 4,
        check_vma=False,
    )
```

```python
import functools
import math

import jax
import jax.numpy as jnp
from jax import lax
from jax.experimental import pallas as pl
from jax.experimental.pallas import tpu as pltpu
from jax.sharding import Mesh
from jax.sharding import PartitionSpec as P

D = 7168
ITERS = 3
ROWS = 112
R = 384
L = 576
LP = 640
T = 128
DP = 64
SLABS = 15
PIECE = 16

COEF_A = 3.4445
COEF_B = -4.775
COEF_C = 2.0315
BETA = 0.95
EPSILON = 1e-07
BF = jnp.bfloat16
F32 = jnp.float32

VMEM = pl.BlockSpec(memory_space=pltpu.VMEM)
PARAMS = pltpu.CompilerParams(vmem_limit_bytes=48 * 1024 * 1024)


def dot(left, right):
    return jnp.dot(left, right, preferred_element_type=F32)


def iota(shape, dim):
    return lax.broadcasted_iota(jnp.int32, shape, dim)


def chip_sum_kernel(mine, other, out):
    total = (mine[...] + other[...]).astype(BF)
    for copy in range(4):
        out[copy] = total


def split3(value):
    high = value.astype(BF).astype(F32)
    rest = value - high
    middle = rest.astype(BF).astype(F32)
    return high, middle, rest - middle


def gram_kernel(parts, moment_r, moment_l, fresh_r, fresh_l, nest_r, nest_l, payload, slabs):
    core = lax.axis_index("core")
    squares = []
    grams = []
    for first, width, moment, new, nest in (
        (0, R, moment_r, fresh_r, nest_r),
        (R, L, moment_l, fresh_l, nest_l),
    ):
        part = [parts[k, :, first : first + width].astype(F32) for k in range(4)]
        summed = (part[0] + part[1]) + (part[2] + part[3])
        fresh = BETA * moment[...] + summed
        nesterov = summed + BETA * fresh
        new[...] = fresh
        nest[...] = nesterov
        squares.append(jnp.sum(nesterov * nesterov))
        low = nesterov.astype(BF)
        if width == L:
            low = jnp.concatenate([low, jnp.zeros((ROWS, LP - L), BF)], axis=1)
        gram = lax.dot_general(low, low, (((0,), (0,)), ((), ())), preferred_element_type=F32)
        grams.append(gram)

    def tile(k, i, j):
        return grams[k][T * i : T * (i + 1), T * j : T * (j + 1)]

    row, lane = iota((T, T), 0), iota((T, T), 1)

    def fold(upper, lower):
        return jnp.where(row <= lane, upper, lower)

    half = iota((64, T), 1) < 64
    last = tile(0, 2, 2)
    corner = jnp.where(half, tile(1, 4, 4)[:64], last[64:])
    tiles = [
        tile(0, 0, 1),
        tile(0, 0, 2),
        tile(0, 1, 2),
        fold(tile(0, 0, 0), tile(0, 1, 1)),
        jnp.concatenate([last[:64], corner], axis=0),
        tile(1, 0, 1),
        tile(1, 0, 2),
        tile(1, 0, 3),
        tile(1, 1, 2),
        tile(1, 1, 3),
        tile(1, 2, 3),
        fold(tile(1, 0, 0), tile(1, 1, 1)),
        fold(tile(1, 2, 2), tile(1, 3, 3)),
    ]
    pieces = [t[64 * h : 64 * (h + 1)] for t in tiles for h in range(2)]
    pieces += [grams[1][512:576, T * j : T * (j + 1)] for j in range(4)]

    parts6 = split3(squares[0]) + split3(squares[1])
    lane1 = iota((64, T), 1)
    row1 = iota((64, T), 0)
    extra = jnp.zeros((64, T), F32)
    for k in range(6):
        extra = jnp.where(lane1 == k, parts6[k], extra)
    for k, (which, i) in enumerate(((0, 1), (1, 1), (1, 3))):
        diagonal = jnp.sum(jnp.where(row == lane, tile(which, i, i), 0.0), axis=0, keepdims=True)
        low_half = pltpu.roll(diagonal, 64, 1)
        extra = jnp.where((row1 == 2 * k) & (lane1 >= 64), low_half, extra)
        extra = jnp.where((row1 == 2 * k + 1) & (lane1 >= 64), diagonal, extra)

    for c in range(2):

        @pl.when(core == c)
        def _():
            for s in range(SLABS):
                slabs[pl.ds(s, DP, stride=PIECE), :] = pieces[SLABS * (1 - c) + s]

    slabs[pl.ds(SLABS, DP, stride=PIECE), :] = extra
    payload[...] = slabs[...].astype(BF)


def scale_kernel(pieces, low, magnitude):
    core, here = lax.axis_index("core"), lax.axis_index("dp")
    total = jnp.sum(pieces[...].reshape(DP, PIECE, T).astype(F32), axis=0)
    last = total[SLABS : SLABS + 1]
    lane1 = iota((1, T), 1)
    router = jnp.sum(jnp.where(lane1 < 3, last, 0.0), axis=1, keepdims=True)
    latent = jnp.sum(jnp.where((lane1 >= 3) & (lane1 < 6), last, 0.0), axis=1, keepdims=True)
    router = jnp.sqrt(router) + EPSILON
    latent = jnp.sqrt(latent) + EPSILON
    inverse_r = 1.0 / (router * router)
    inverse_l = 1.0 / (latent * latent)
    row, lane = iota((PIECE, T), 0), iota((PIECE, T), 1)
    slab = SLABS * (1 - core) + row
    of_router = (slab < 9) | ((slab == 9) & (lane >= 64))
    of_router = jnp.where(row == SLABS, jnp.where(here < 2, 1, 0), jnp.where(of_router, 1, 0))
    scaled = (total * jnp.where(of_router == 1, inverse_r, inverse_l)).astype(BF)
    for k in range(DP):
        low[PIECE * k : PIECE * (k + 1), :] = scaled
    magnitude[...] = jnp.where(iota((8, T), 0) == 0, router, latent)


def unpacker(halves):
    row, lane = iota((T, T), 0), iota((T, T), 1)
    lane1 = iota((1, T), 1)
    extra = halves[0, pl.ds(SLABS, 8, stride=PIECE), :]

    def slab(g):
        return halves[g // SLABS, pl.ds(g % SLABS, DP, stride=PIECE), :]

    def tile(t):
        return jnp.concatenate([slab(2 * t), slab(2 * t + 1)], axis=0)

    def put(ref, i, j, value):
        ref[T * i : T * (i + 1), T * j : T * (j + 1)] = value.astype(BF)

    def both(ref, i, j, t):
        value = tile(t)
        put(ref, i, j, value)
        put(ref, j, i, value.T)

    def unfold(ref, i, j, t, k):
        value = tile(t)
        flipped = value.T
        put(ref, i, i, jnp.where(row <= lane, value, flipped))
        low_half = pltpu.roll(extra[2 * k : 2 * k + 1], 64, 1)
        diagonal = jnp.where(lane1 < 64, low_half, extra[2 * k + 1 : 2 * k + 2])
        inner = jnp.where(row > lane, value, flipped)
        put(ref, j, j, jnp.where(row == lane, diagonal, inner))

    return slab, tile, put, both, unfold


def product(left, right, rows, width, epilogue, symmetric=False):
    edge = (rows - 1) // 256 * 256 if symmetric else width
    for start in range(0, edge, 256):
        stop = min(start + 256, edge)
        acc = dot(left[:rows, :], right[:, start:stop])
        for ref, value in epilogue(acc, 0, start, stop):
            ref[:rows, start:stop] = value
            if symmetric:
                strip = value[edge:rows].astype(F32)
                if rows - edge < T:
                    strip = jnp.concatenate([strip, jnp.zeros((T + edge - rows, 256), F32)], axis=0)
                ref[start:stop, edge:width] = strip.T.astype(BF)
    if symmetric:
        acc = dot(left[edge:rows, :], right[:, edge:width])
        for ref, value in epilogue(acc, edge, edge, width):
            ref[edge:rows, edge:width] = value


def chain(gram, step, mix, fac, tmp, rows, width, symmetric):
    def store(ref):
        return lambda acc, top, start, stop: [(ref, acc.astype(BF))]

    def mixture(now, acc, top, start, stop):
        squared = acc.astype(BF).astype(F32)
        value = COEF_B * now[top : top + acc.shape[0], start:stop].astype(F32) + COEF_C * squared
        return value.astype(BF)

    def begin(acc, top, start, stop):
        value = mixture(gram, acc, top, start, stop)
        eye = (iota(acc.shape, 0) + top == iota(acc.shape, 1) + start).astype(F32)
        return [(fac, (COEF_A * eye + value.astype(F32)).astype(BF))]

    product(gram, gram, rows, width, begin, True)
    for iteration in range(1, ITERS):

        def mixing(acc, top, start, stop):
            return [(mix, mixture(step, acc, top, start, stop))]

        def blend(acc, top, start, stop, fac=fac, tmp=tmp):
            value = COEF_A * fac[top : top + acc.shape[0], start:stop].astype(F32) + acc
            return [(tmp, value.astype(BF))]

        product(fac, gram, rows, width, store(tmp), symmetric and iteration == 1)
        product(tmp, fac, rows, width, store(step), symmetric)
        product(step, step, rows, width, mixing, symmetric)
        product(mix, fac, rows, width, blend, symmetric)
        fac, tmp = tmp, fac
    return fac


def router_kernel(mine, out, half, gram, step, mix, fac, tmp):
    out[: DP * PIECE, :] = mine[...]

    @pl.when(lax.axis_index("core") == 1)
    def _():
        half[0] = mine[...].astype(F32)
        slab, tile, put, both, unfold = unpacker(half)
        both(gram, 0, 1, 0)
        both(gram, 0, 2, 1)
        both(gram, 1, 2, 2)
        unfold(gram, 0, 1, 3, 0)
        last = tile(4)
        upper = iota((T, T), 0) <= iota((T, T), 1)
        put(gram, 2, 2, jnp.where(upper, last, last.T))
        factor = chain(gram, step, mix, fac, tmp, R, R, False)
        for j in range(R // T):
            first = DP * PIECE + R * j
            out[first : first + R, :] = factor[:, T * j : T * (j + 1)]


def update_kernel(
    mine, other, magnitude, nest_r, nest_l, fresh_r, fresh_l, new_r, new_l, out_r, out_l,
    halves, gram, step, mix, fac, tmp, fac_r, value_r, value_l, sems,
):
    copies = []

    def write(source, target):
        copies.append(pltpu.make_async_copy(source, target, sems.at[len(copies)]))
        copies[-1].start()

    write(fresh_r, new_r)
    write(fresh_l, new_l)

    first = lax.axis_index("core") == 1
    a, b = mine[: DP * PIECE, :].astype(F32), other[: DP * PIECE, :].astype(F32)
    halves[0] = jnp.where(first, a, b)
    halves[1] = jnp.where(first, b, a)
    slab, tile, put, both, unfold = unpacker(halves)
    gram[L:, :] = jnp.zeros((LP - L, LP), BF)
    gram[512:L, 512:] = jnp.where(iota((64, T), 1) < 64, slab(9), 0.0).astype(BF)
    both(gram, 0, 1, 5)
    both(gram, 0, 2, 6)
    both(gram, 0, 3, 7)
    both(gram, 1, 2, 8)
    both(gram, 1, 3, 9)
    both(gram, 2, 3, 10)
    unfold(gram, 0, 1, 11, 1)
    unfold(gram, 2, 3, 12, 2)
    for j in range(4):
        strip = jnp.concatenate([slab(26 + j), jnp.zeros((64, T), F32)], axis=0)
        gram[512:L, T * j : T * (j + 1)] = strip[:64].astype(BF)
        put(gram, j, 4, strip.T)
    for ref in (step, mix, fac, tmp):
        ref[L:, :] = jnp.zeros((LP - L, LP), BF)

    root = math.sqrt(D)
    contract = (((1,), (1,)), ((), ()))

    def apply(nest, magnitude, factor, rows, width, value, out):
        scaled = (nest[...] / magnitude).astype(BF)
        if width > rows:
            scaled = jnp.concatenate([scaled, jnp.zeros((ROWS, width - rows), BF)], axis=1)
        for start in range(0, rows, 256):
            stop = min(start + 256, rows)
            part = lax.dot_general(
                scaled, factor[start:stop, :], contract, preferred_element_type=F32
            )
            value[:, start:stop] = part * root
            write(value.at[:, start:stop], out.at[:, start:stop])

    for j in range(R // T):
        rows = slice(DP * PIECE + R * j, DP * PIECE + R * (j + 1))
        fac_r[:, T * j : T * (j + 1)] = jnp.where(first, mine[rows, :], other[rows, :])
    apply(nest_r, magnitude[0:1, 0:1], fac_r, R, R, value_r, out_r)
    factor = chain(gram, step, mix, fac, tmp, L, LP, True)
    apply(nest_l, magnitude[1:2, 0:1], factor, L, LP, value_l, out_l)
    for copy in copies:
        copy.wait()


def call(kernel, out_shape, scratch, name, *args):
    return pl.pallas_call(
        kernel,
        out_shape=out_shape,
        in_specs=[VMEM] * len(args),
        out_specs=jax.tree.map(lambda _: VMEM, out_shape),
        scratch_shapes=scratch,
        compiler_params=PARAMS,
        name=name,
    )(*args)


def router_call(mine):
    return call(
        router_kernel,
        jax.ShapeDtypeStruct((DP * PIECE + R * R // T, T), BF),
        [pltpu.VMEM((1, DP * PIECE, T), F32)] + [pltpu.VMEM((R, R), BF)] * 5,
        "router_chain", mine,
    )


def chain_call(mine, other, magnitude, nest_r, nest_l, fresh_r, fresh_l):
    shape = jax.ShapeDtypeStruct
    return pl.pallas_call(
        update_kernel,
        out_shape=(shape((ROWS, R), F32), shape((ROWS, L), F32)) * 2,
        in_specs=[VMEM] * 7,
        out_specs=[pl.BlockSpec(memory_space=pl.ANY)] * 4,
        scratch_shapes=[pltpu.VMEM((2, DP * PIECE, T), F32)]
        + [pltpu.VMEM((LP, LP), BF)] * 5
        + [pltpu.VMEM((R, R), BF), pltpu.VMEM((ROWS, R), F32), pltpu.VMEM((ROWS, L), F32)]
        + [pltpu.SemaphoreType.DMA((7,))],
        compiler_params=PARAMS,
        name="chain_apply",
    )(mine, other, magnitude, nest_r, nest_l, fresh_r, fresh_l)


def local(router_grads, latent_grads, router_moment, latent_moment):
    shape = jax.ShapeDtypeStruct
    swap = [(0, 1), (1, 0)]
    grads = lax.optimization_barrier(jnp.concatenate([router_grads[0], latent_grads[0]], axis=1))
    other = lax.ppermute(grads, "core", swap)
    chip = call(chip_sum_kernel, shape((4, ROWS, R + L), BF), [], "chip_sum", grads, other)
    parts = lax.all_to_all(chip, "x", 0, 0)
    fresh_r, fresh_l, nest_r, nest_l, payload = call(
        gram_kernel,
        (
            shape((ROWS, R), F32), shape((ROWS, L), F32),
            shape((ROWS, R), F32), shape((ROWS, L), F32),
            shape((DP * PIECE, T), BF),
        ),
        [pltpu.VMEM((DP * PIECE, T), F32)], "momentum_gram", parts, router_moment, latent_moment,
    )
    pieces = lax.all_to_all(payload.reshape(DP, PIECE, T), "dp", 0, 0)
    low, magnitude = call(
        scale_kernel,
        (shape((DP * PIECE, T), BF), shape((8, T), F32)),
        [], "scale_gram", pieces.reshape(DP * PIECE, T),
    )
    mine = lax.all_to_all(low.reshape(DP, PIECE, T), "dp", 0, 0).reshape(DP * PIECE, T)
    mine = router_call(mine)
    other = lax.ppermute(mine, "core", swap)
    return chain_call(mine, other, magnitude, nest_r, nest_l, fresh_r, fresh_l)


def solution(mesh):
    inner = Mesh(mesh.devices.reshape(DP, 4, 2), ("dp", "x", "core"))
    group = ("x", "core")
    return jax.shard_map(
        local,
        mesh=inner,
        in_specs=(P(group, "dp", None), P(group, "dp", None), P("dp", None), P("dp", None)),
        out_specs=(P("dp", None),) * 4,
        check_vma=False,
    )
```

```python
import functools
import math

import jax
import jax.numpy as jnp
from jax import lax
from jax.experimental import pallas as pl
from jax.experimental.pallas import tpu as pltpu
from jax.sharding import Mesh
from jax.sharding import PartitionSpec as P

D = 7168
ITERS = 3
ROWS = 112
R = 384
L = 576
LP = 640
T = 128
DP = 64
SLABS = 15
PIECE = 16

COEF_A = 3.4445
COEF_B = -4.775
COEF_C = 2.0315
BETA = 0.95
EPSILON = 1e-07
BF = jnp.bfloat16
F32 = jnp.float32

VMEM = pl.BlockSpec(memory_space=pltpu.VMEM)
PARAMS = pltpu.CompilerParams(vmem_limit_bytes=48 * 1024 * 1024)


def dot(left, right):
    return jnp.dot(left, right, preferred_element_type=F32)


def iota(shape, dim):
    return lax.broadcasted_iota(jnp.int32, shape, dim)


def chip_sum_kernel(mine, other, out):
    total = (mine[...] + other[...]).astype(BF)
    for copy in range(4):
        out[copy] = total


def split3(value):
    high = value.astype(BF).astype(F32)
    rest = value - high
    middle = rest.astype(BF).astype(F32)
    return high, middle, rest - middle


def gram_kernel(parts, moment_r, moment_l, fresh_r, fresh_l, nest_r, nest_l, payload, slabs):
    core = lax.axis_index("core")
    squares = []
    grams = []
    for first, width, moment, new, nest in (
        (0, R, moment_r, fresh_r, nest_r),
        (R, L, moment_l, fresh_l, nest_l),
    ):
        part = [parts[k, :, first : first + width].astype(F32) for k in range(4)]
        summed = (part[0] + part[1]) + (part[2] + part[3])
        fresh = BETA * moment[...] + summed
        nesterov = summed + BETA * fresh
        new[...] = fresh
        nest[...] = nesterov
        squares.append(jnp.sum(nesterov * nesterov))
        low = nesterov.astype(BF)
        if width == L:
            low = jnp.concatenate([low, jnp.zeros((ROWS, LP - L), BF)], axis=1)
        gram = lax.dot_general(low, low, (((0,), (0,)), ((), ())), preferred_element_type=F32)
        grams.append(gram)

    def tile(k, i, j):
        return grams[k][T * i : T * (i + 1), T * j : T * (j + 1)]

    row, lane = iota((T, T), 0), iota((T, T), 1)

    def fold(upper, lower):
        return jnp.where(row <= lane, upper, lower)

    half = iota((64, T), 1) < 64
    last = tile(0, 2, 2)
    corner = jnp.where(half, tile(1, 4, 4)[:64], last[64:])
    tiles = [
        tile(0, 0, 1),
        tile(0, 0, 2),
        tile(0, 1, 2),
        fold(tile(0, 0, 0), tile(0, 1, 1)),
        jnp.concatenate([last[:64], corner], axis=0),
        tile(1, 0, 1),
        tile(1, 0, 2),
        tile(1, 0, 3),
        tile(1, 1, 2),
        tile(1, 1, 3),
        tile(1, 2, 3),
        fold(tile(1, 0, 0), tile(1, 1, 1)),
        fold(tile(1, 2, 2), tile(1, 3, 3)),
    ]
    pieces = [t[64 * h : 64 * (h + 1)] for t in tiles for h in range(2)]
    pieces += [grams[1][512:576, T * j : T * (j + 1)] for j in range(4)]

    parts6 = split3(squares[0]) + split3(squares[1])
    lane1 = iota((64, T), 1)
    row1 = iota((64, T), 0)
    extra = jnp.zeros((64, T), F32)
    for k in range(6):
        extra = jnp.where(lane1 == k, parts6[k], extra)
    for k, (which, i) in enumerate(((0, 1), (1, 1), (1, 3))):
        diagonal = jnp.sum(jnp.where(row == lane, tile(which, i, i), 0.0), axis=0, keepdims=True)
        low_half = pltpu.roll(diagonal, 64, 1)
        extra = jnp.where((row1 == 2 * k) & (lane1 >= 64), low_half, extra)
        extra = jnp.where((row1 == 2 * k + 1) & (lane1 >= 64), diagonal, extra)

    for c in range(2):

        @pl.when(core == c)
        def _():
            for s in range(SLABS):
                slabs[pl.ds(s, DP, stride=PIECE), :] = pieces[SLABS * (1 - c) + s]

    slabs[pl.ds(SLABS, DP, stride=PIECE), :] = extra
    payload[...] = slabs[...].astype(BF)


def scale_kernel(pieces, low, magnitude):
    core, here = lax.axis_index("core"), lax.axis_index("dp")
    total = jnp.sum(pieces[...].reshape(DP, PIECE, T).astype(F32), axis=0)
    last = total[SLABS : SLABS + 1]
    lane1 = iota((1, T), 1)
    router = jnp.sum(jnp.where(lane1 < 3, last, 0.0), axis=1, keepdims=True)
    latent = jnp.sum(jnp.where((lane1 >= 3) & (lane1 < 6), last, 0.0), axis=1, keepdims=True)
    router = jnp.sqrt(router) + EPSILON
    latent = jnp.sqrt(latent) + EPSILON
    inverse_r = 1.0 / (router * router)
    inverse_l = 1.0 / (latent * latent)
    row, lane = iota((PIECE, T), 0), iota((PIECE, T), 1)
    slab = SLABS * (1 - core) + row
    of_router = (slab < 9) | ((slab == 9) & (lane >= 64))
    of_router = jnp.where(row == SLABS, jnp.where(here < 2, 1, 0), jnp.where(of_router, 1, 0))
    scaled = (total * jnp.where(of_router == 1, inverse_r, inverse_l)).astype(BF)
    for k in range(DP):
        low[PIECE * k : PIECE * (k + 1), :] = scaled
    magnitude[...] = jnp.where(iota((8, T), 0) == 0, router, latent)


def unpacker(halves):
    row, lane = iota((T, T), 0), iota((T, T), 1)
    lane1 = iota((1, T), 1)
    extra = halves[0, pl.ds(SLABS, 8, stride=PIECE), :]

    def slab(g):
        return halves[g // SLABS, pl.ds(g % SLABS, DP, stride=PIECE), :]

    def tile(t):
        return jnp.concatenate([slab(2 * t), slab(2 * t + 1)], axis=0)

    def put(ref, i, j, value):
        ref[T * i : T * (i + 1), T * j : T * (j + 1)] = value.astype(BF)

    def both(ref, i, j, t):
        value = tile(t)
        put(ref, i, j, value)
        put(ref, j, i, value.T)

    def unfold(ref, i, j, t, k):
        value = tile(t)
        flipped = value.T
        put(ref, i, i, jnp.where(row <= lane, value, flipped))
        low_half = pltpu.roll(extra[2 * k : 2 * k + 1], 64, 1)
        diagonal = jnp.where(lane1 < 64, low_half, extra[2 * k + 1 : 2 * k + 2])
        inner = jnp.where(row > lane, value, flipped)
        put(ref, j, j, jnp.where(row == lane, diagonal, inner))

    return slab, tile, put, both, unfold


def strips(left, right, rows, width, epilogue, symmetric=False):
    edge = (rows - 1) // 256 * 256 if symmetric else width
    for start in range(0, edge, 256):
        stop = min(start + 256, edge)
        acc = dot(left[:rows, :], right[:, start:stop])
        for ref, value in epilogue(acc, 0, start, stop):
            ref[:rows, start:stop] = value
            if symmetric:
                strip = value[edge:rows].astype(F32)
                if rows - edge < T:
                    strip = jnp.concatenate([strip, jnp.zeros((T + edge - rows, 256), F32)], axis=0)
                ref[start:stop, edge:width] = strip.T.astype(BF)
    if symmetric:
        acc = dot(left[edge:rows, :], right[:, edge:width])
        for ref, value in epilogue(acc, edge, edge, width):
            ref[edge:rows, edge:width] = value


def product(left, right, rows, width, epilogue, symmetric=0):
    for start in range(0, width, 256):
        stop = min(start + 256, width)
        top = start if symmetric else 0
        acc = dot(left[top:rows, :], right[:, start:stop])
        for ref, value in epilogue(acc, top, start, stop):
            ref[top:rows, start:stop] = value
            if symmetric and stop < width:
                below = value[stop - top :].astype(F32)
                if rows < width:
                    below = jnp.concatenate([below, jnp.zeros((width - rows, 256), F32)], axis=0)
                ref[start:stop, stop:width] = below.T.astype(BF)


def chain(gram, step, mix, fac, tmp, rows, width, symmetric):
    def store(ref):
        return lambda acc, top, start, stop: [(ref, acc.astype(BF))]

    def mixture(now, acc, top, start, stop):
        squared = acc.astype(BF).astype(F32)
        value = COEF_B * now[top : top + acc.shape[0], start:stop].astype(F32) + COEF_C * squared
        return value.astype(BF)

    def begin(acc, top, start, stop):
        value = mixture(gram, acc, top, start, stop)
        eye = (iota(acc.shape, 0) + top == iota(acc.shape, 1) + start).astype(F32)
        return [(fac, (COEF_A * eye + value.astype(F32)).astype(BF))]

    product(gram, gram, rows, width, begin, True)
    for iteration in range(1, ITERS):

        def mixing(acc, top, start, stop):
            return [(mix, mixture(step, acc, top, start, stop))]

        def blend(acc, top, start, stop, fac=fac, tmp=tmp):
            value = COEF_A * fac[top : top + acc.shape[0], start:stop].astype(F32) + acc
            return [(tmp, value.astype(BF))]

        strips(fac, gram, rows, width, store(tmp), symmetric and iteration == 1)
        strips(tmp, fac, rows, width, store(step), symmetric)
        strips(step, step, rows, width, mixing, symmetric)
        strips(mix, fac, rows, width, blend, symmetric)
        fac, tmp = tmp, fac
    return fac


def router_kernel(mine, out, half, gram, step, mix, fac, tmp):
    out[: DP * PIECE, :] = mine[...]

    @pl.when(lax.axis_index("core") == 1)
    def _():
        half[0] = mine[...].astype(F32)
        slab, tile, put, both, unfold = unpacker(half)
        both(gram, 0, 1, 0)
        both(gram, 0, 2, 1)
        both(gram, 1, 2, 2)
        unfold(gram, 0, 1, 3, 0)
        last = tile(4)
        upper = iota((T, T), 0) <= iota((T, T), 1)
        put(gram, 2, 2, jnp.where(upper, last, last.T))
        factor = chain(gram, step, mix, fac, tmp, R, R, False)
        for j in range(R // T):
            first = DP * PIECE + R * j
            out[first : first + R, :] = factor[:, T * j : T * (j + 1)]


def update_kernel(
    mine, other, magnitude, nest_r, nest_l, fresh_r, fresh_l, new_r, new_l, out_r, out_l,
    halves, gram, step, mix, fac, tmp, fac_r, value_r, value_l, sems,
):
    copies = []

    def write(source, target):
        copies.append(pltpu.make_async_copy(source, target, sems.at[len(copies)]))
        copies[-1].start()

    write(fresh_r, new_r)
    write(fresh_l, new_l)

    first = lax.axis_index("core") == 1
    a, b = mine[: DP * PIECE, :].astype(F32), other[: DP * PIECE, :].astype(F32)
    halves[0] = jnp.where(first, a, b)
    halves[1] = jnp.where(first, b, a)
    slab, tile, put, both, unfold = unpacker(halves)
    gram[L:, :] = jnp.zeros((LP - L, LP), BF)
    gram[512:L, 512:] = jnp.where(iota((64, T), 1) < 64, slab(9), 0.0).astype(BF)
    both(gram, 0, 1, 5)
    both(gram, 0, 2, 6)
    both(gram, 0, 3, 7)
    both(gram, 1, 2, 8)
    both(gram, 1, 3, 9)
    both(gram, 2, 3, 10)
    unfold(gram, 0, 1, 11, 1)
    unfold(gram, 2, 3, 12, 2)
    for j in range(4):
        strip = jnp.concatenate([slab(26 + j), jnp.zeros((64, T), F32)], axis=0)
        gram[512:L, T * j : T * (j + 1)] = strip[:64].astype(BF)
        put(gram, j, 4, strip.T)
    for ref in (step, mix, fac, tmp):
        ref[L:, :] = jnp.zeros((LP - L, LP), BF)

    root = math.sqrt(D)
    contract = (((1,), (1,)), ((), ()))

    def apply(nest, magnitude, factor, rows, width, value, out):
        scaled = (nest[...] / magnitude).astype(BF)
        if width > rows:
            scaled = jnp.concatenate([scaled, jnp.zeros((ROWS, width - rows), BF)], axis=1)
        for start in range(0, rows, 256):
            stop = min(start + 256, rows)
            part = lax.dot_general(
                scaled, factor[start:stop, :], contract, preferred_element_type=F32
            )
            value[:, start:stop] = part * root
            write(value.at[:, start:stop], out.at[:, start:stop])

    for j in range(R // T):
        rows = slice(DP * PIECE + R * j, DP * PIECE + R * (j + 1))
        fac_r[:, T * j : T * (j + 1)] = jnp.where(first, mine[rows, :], other[rows, :])
    apply(nest_r, magnitude[0:1, 0:1], fac_r, R, R, value_r, out_r)
    factor = chain(gram, step, mix, fac, tmp, L, LP, True)
    apply(nest_l, magnitude[1:2, 0:1], factor, L, LP, value_l, out_l)
    for copy in copies:
        copy.wait()


def call(kernel, out_shape, scratch, name, *args):
    return pl.pallas_call(
        kernel,
        out_shape=out_shape,
        in_specs=[VMEM] * len(args),
        out_specs=jax.tree.map(lambda _: VMEM, out_shape),
        scratch_shapes=scratch,
        compiler_params=PARAMS,
        name=name,
    )(*args)


def router_call(mine):
    return call(
        router_kernel,
        jax.ShapeDtypeStruct((DP * PIECE + R * R // T, T), BF),
        [pltpu.VMEM((1, DP * PIECE, T), F32)] + [pltpu.VMEM((R, R), BF)] * 5,
        "router_chain", mine,
    )


def chain_call(mine, other, magnitude, nest_r, nest_l, fresh_r, fresh_l):
    shape = jax.ShapeDtypeStruct
    return pl.pallas_call(
        update_kernel,
        out_shape=(shape((ROWS, R), F32), shape((ROWS, L), F32)) * 2,
        in_specs=[VMEM] * 7,
        out_specs=[pl.BlockSpec(memory_space=pl.ANY)] * 4,
        scratch_shapes=[pltpu.VMEM((2, DP * PIECE, T), F32)]
        + [pltpu.VMEM((LP, LP), BF)] * 5
        + [pltpu.VMEM((R, R), BF), pltpu.VMEM((ROWS, R), F32), pltpu.VMEM((ROWS, L), F32)]
        + [pltpu.SemaphoreType.DMA((7,))],
        compiler_params=PARAMS,
        name="chain_apply",
    )(mine, other, magnitude, nest_r, nest_l, fresh_r, fresh_l)


def local(router_grads, latent_grads, router_moment, latent_moment):
    shape = jax.ShapeDtypeStruct
    swap = [(0, 1), (1, 0)]
    grads = lax.optimization_barrier(jnp.concatenate([router_grads[0], latent_grads[0]], axis=1))
    other = lax.ppermute(grads, "core", swap)
    chip = call(chip_sum_kernel, shape((4, ROWS, R + L), BF), [], "chip_sum", grads, other)
    parts = lax.all_to_all(chip, "x", 0, 0)
    fresh_r, fresh_l, nest_r, nest_l, payload = call(
        gram_kernel,
        (
            shape((ROWS, R), F32), shape((ROWS, L), F32),
            shape((ROWS, R), F32), shape((ROWS, L), F32),
            shape((DP * PIECE, T), BF),
        ),
        [pltpu.VMEM((DP * PIECE, T), F32)], "momentum_gram", parts, router_moment, latent_moment,
    )
    pieces = lax.all_to_all(payload.reshape(DP, PIECE, T), "dp", 0, 0)
    low, magnitude = call(
        scale_kernel,
        (shape((DP * PIECE, T), BF), shape((8, T), F32)),
        [], "scale_gram", pieces.reshape(DP * PIECE, T),
    )
    mine = lax.all_to_all(low.reshape(DP, PIECE, T), "dp", 0, 0).reshape(DP * PIECE, T)
    mine = router_call(mine)
    other = lax.ppermute(mine, "core", swap)
    return chain_call(mine, other, magnitude, nest_r, nest_l, fresh_r, fresh_l)


def solution(mesh):
    inner = Mesh(mesh.devices.reshape(DP, 4, 2), ("dp", "x", "core"))
    group = ("x", "core")
    return jax.shard_map(
        local,
        mesh=inner,
        in_specs=(P(group, "dp", None), P(group, "dp", None), P("dp", None), P("dp", None)),
        out_specs=(P("dp", None),) * 4,
        check_vma=False,
    )
```

```python
import functools
import math

import jax
import jax.numpy as jnp
from jax import lax
from jax.experimental import pallas as pl
from jax.experimental.pallas import tpu as pltpu
from jax.sharding import Mesh
from jax.sharding import PartitionSpec as P

D = 7168
ITERS = 3
ROWS = 112
R = 384
L = 576
LP = 640
T = 128
DP = 64
SLABS = 15
PIECE = 16

COEF_A = 3.4445
COEF_B = -4.775
COEF_C = 2.0315
BETA = 0.95
EPSILON = 1e-07
BF = jnp.bfloat16
F32 = jnp.float32

VMEM = pl.BlockSpec(memory_space=pltpu.VMEM)
PARAMS = pltpu.CompilerParams(vmem_limit_bytes=48 * 1024 * 1024)


def dot(left, right):
    return jnp.dot(left, right, preferred_element_type=F32)


def iota(shape, dim):
    return lax.broadcasted_iota(jnp.int32, shape, dim)


def chip_sum_kernel(mine, other, out):
    out[...] = (mine[...] + other[...]).astype(BF)


def split3(value):
    high = value.astype(BF).astype(F32)
    rest = value - high
    middle = rest.astype(BF).astype(F32)
    return high, middle, rest - middle


def gram_kernel(parts, moment_r, moment_l, fresh_r, fresh_l, nest_r, nest_l, payload, slabs):
    core = lax.axis_index("core")
    squares = []
    grams = []
    for first, width, moment, new, nest in (
        (0, R, moment_r, fresh_r, nest_r),
        (R, L, moment_l, fresh_l, nest_l),
    ):
        part = [parts[k, :, first : first + width].astype(F32) for k in range(4)]
        summed = (part[0] + part[1]) + (part[2] + part[3])
        fresh = BETA * moment[...] + summed
        nesterov = summed + BETA * fresh
        new[...] = fresh
        nest[...] = nesterov
        squares.append(jnp.sum(nesterov * nesterov))
        low = nesterov.astype(BF)
        if width == L:
            low = jnp.concatenate([low, jnp.zeros((ROWS, LP - L), BF)], axis=1)
        gram = lax.dot_general(low, low, (((0,), (0,)), ((), ())), preferred_element_type=F32)
        grams.append(gram)

    def tile(k, i, j):
        return grams[k][T * i : T * (i + 1), T * j : T * (j + 1)]

    row, lane = iota((T, T), 0), iota((T, T), 1)

    def fold(upper, lower):
        return jnp.where(row <= lane, upper, lower)

    half = iota((64, T), 1) < 64
    last = tile(0, 2, 2)
    corner = jnp.where(half, tile(1, 4, 4)[:64], last[64:])
    tiles = [
        tile(0, 0, 1),
        tile(0, 0, 2),
        tile(0, 1, 2),
        fold(tile(0, 0, 0), tile(0, 1, 1)),
        jnp.concatenate([last[:64], corner], axis=0),
        tile(1, 0, 1),
        tile(1, 0, 2),
        tile(1, 0, 3),
        tile(1, 1, 2),
        tile(1, 1, 3),
        tile(1, 2, 3),
        fold(tile(1, 0, 0), tile(1, 1, 1)),
        fold(tile(1, 2, 2), tile(1, 3, 3)),
    ]
    pieces = [t[64 * h : 64 * (h + 1)] for t in tiles for h in range(2)]
    pieces += [grams[1][512:576, T * j : T * (j + 1)] for j in range(4)]

    parts6 = split3(squares[0]) + split3(squares[1])
    lane1 = iota((64, T), 1)
    row1 = iota((64, T), 0)
    extra = jnp.zeros((64, T), F32)
    for k in range(6):
        extra = jnp.where(lane1 == k, parts6[k], extra)
    for k, (which, i) in enumerate(((0, 1), (1, 1), (1, 3))):
        diagonal = jnp.sum(jnp.where(row == lane, tile(which, i, i), 0.0), axis=0, keepdims=True)
        low_half = pltpu.roll(diagonal, 64, 1)
        extra = jnp.where((row1 == 2 * k) & (lane1 >= 64), low_half, extra)
        extra = jnp.where((row1 == 2 * k + 1) & (lane1 >= 64), diagonal, extra)

    for c in range(2):

        @pl.when(core == c)
        def _():
            for s in range(SLABS):
                slabs[pl.ds(s, DP, stride=PIECE), :] = pieces[SLABS * (1 - c) + s]

    slabs[pl.ds(SLABS, DP, stride=PIECE), :] = extra
    payload[...] = slabs[...].astype(BF)


def scale_kernel(pieces, low, magnitude):
    core, here = lax.axis_index("core"), lax.axis_index("dp")
    total = jnp.sum(pieces[...].reshape(DP, PIECE, T).astype(F32), axis=0)
    last = total[SLABS : SLABS + 1]
    lane1 = iota((1, T), 1)
    router = jnp.sum(jnp.where(lane1 < 3, last, 0.0), axis=1, keepdims=True)
    latent = jnp.sum(jnp.where((lane1 >= 3) & (lane1 < 6), last, 0.0), axis=1, keepdims=True)
    router = jnp.sqrt(router) + EPSILON
    latent = jnp.sqrt(latent) + EPSILON
    inverse_r = 1.0 / (router * router)
    inverse_l = 1.0 / (latent * latent)
    row, lane = iota((PIECE, T), 0), iota((PIECE, T), 1)
    slab = SLABS * (1 - core) + row
    of_router = (slab < 9) | ((slab == 9) & (lane >= 64))
    of_router = jnp.where(row == SLABS, jnp.where(here < 2, 1, 0), jnp.where(of_router, 1, 0))
    scaled = (total * jnp.where(of_router == 1, inverse_r, inverse_l)).astype(BF)
    for k in range(DP):
        low[PIECE * k : PIECE * (k + 1), :] = scaled
    magnitude[...] = jnp.where(iota((8, T), 0) == 0, router, latent)


def unpacker(half, early=None):
    row, lane = iota((T, T), 0), iota((T, T), 1)
    lane1 = iota((1, T), 1)
    extra = half[pl.ds(SLABS, 8, stride=PIECE), :]

    def slab(g):
        if early is None:
            return half[pl.ds(g, DP, stride=PIECE), :]
        if g < SLABS:
            return early[DP * (g - 9) : DP * (g - 8), :]
        return half[pl.ds(g - SLABS, DP, stride=PIECE), :]

    def tile(t):
        return jnp.concatenate([slab(2 * t), slab(2 * t + 1)], axis=0)

    def put(ref, i, j, value):
        ref[T * i : T * (i + 1), T * j : T * (j + 1)] = value.astype(BF)

    def both(ref, i, j, t):
        value = tile(t)
        put(ref, i, j, value)
        put(ref, j, i, value.T)

    def unfold(ref, i, j, t, k):
        value = tile(t)
        flipped = value.T
        put(ref, i, i, jnp.where(row <= lane, value, flipped))
        low_half = pltpu.roll(extra[2 * k : 2 * k + 1], 64, 1)
        diagonal = jnp.where(lane1 < 64, low_half, extra[2 * k + 1 : 2 * k + 2])
        inner = jnp.where(row > lane, value, flipped)
        put(ref, j, j, jnp.where(row == lane, diagonal, inner))

    return slab, tile, put, both, unfold


def strips(left, right, rows, width, epilogue, symmetric=False):
    edge = (rows - 1) // 256 * 256 if symmetric else width
    for start in range(0, edge, 256):
        stop = min(start + 256, edge)
        acc = dot(left[:rows, :], right[:, start:stop])
        for ref, value in epilogue(acc, 0, start, stop):
            ref[:rows, start:stop] = value
            if symmetric:
                strip = value[edge:rows].astype(F32)
                if rows - edge < T:
                    strip = jnp.concatenate([strip, jnp.zeros((T + edge - rows, 256), F32)], axis=0)
                ref[start:stop, edge:width] = strip.T.astype(BF)
    if symmetric:
        acc = dot(left[edge:rows, :], right[:, edge:width])
        for ref, value in epilogue(acc, edge, edge, width):
            ref[edge:rows, edge:width] = value


def product(left, right, rows, width, epilogue, symmetric=0):
    for start in range(0, width, 256):
        stop = min(start + 256, width)
        top = start if symmetric else 0
        acc = dot(left[top:rows, :], right[:, start:stop])
        for ref, value in epilogue(acc, top, start, stop):
            ref[top:rows, start:stop] = value
            if symmetric and stop < width:
                below = value[stop - top :].astype(F32)
                if rows < width:
                    below = jnp.concatenate([below, jnp.zeros((width - rows, 256), F32)], axis=0)
                ref[start:stop, stop:width] = below.T.astype(BF)


def chain(gram, step, mix, fac, tmp, rows, width, symmetric):
    def store(ref):
        return lambda acc, top, start, stop: [(ref, acc.astype(BF))]

    def mixture(now, acc, top, start, stop):
        squared = acc.astype(BF).astype(F32)
        value = COEF_B * now[top : top + acc.shape[0], start:stop].astype(F32) + COEF_C * squared
        return value.astype(BF)

    def begin(acc, top, start, stop):
        value = mixture(gram, acc, top, start, stop)
        eye = (iota(acc.shape, 0) + top == iota(acc.shape, 1) + start).astype(F32)
        return [(fac, (COEF_A * eye + value.astype(F32)).astype(BF))]

    product(gram, gram, rows, width, begin, True)
    for iteration in range(1, ITERS):

        def mixing(acc, top, start, stop):
            return [(mix, mixture(step, acc, top, start, stop))]

        def blend(acc, top, start, stop, fac=fac, tmp=tmp):
            value = COEF_A * fac[top : top + acc.shape[0], start:stop].astype(F32) + acc
            return [(tmp, value.astype(BF))]

        strips(fac, gram, rows, width, store(tmp), symmetric and iteration == 1)
        strips(tmp, fac, rows, width, store(step), symmetric)
        strips(step, step, rows, width, mixing, symmetric)
        strips(mix, fac, rows, width, blend, symmetric)
        fac, tmp = tmp, fac
    return fac


def router_kernel(mine, out, half, gram, step, mix, fac, tmp):
    @pl.when(lax.axis_index("core") == 0)
    def _():
        out[: DP * PIECE, :] = mine[...]

    @pl.when(lax.axis_index("core") == 1)
    def _():
        half[...] = mine[...].astype(F32)
        slab, tile, put, both, unfold = unpacker(half)
        both(gram, 0, 1, 0)
        both(gram, 0, 2, 1)
        both(gram, 1, 2, 2)
        unfold(gram, 0, 1, 3, 0)
        last = tile(4)
        upper = iota((T, T), 0) <= iota((T, T), 1)
        put(gram, 2, 2, jnp.where(upper, last, last.T))
        factor = chain(gram, step, mix, fac, tmp, R, R, False)
        for j in range(R // T):
            out[R * j : R * (j + 1), :] = factor[:, T * j : T * (j + 1)]
        for k in range(6):
            out[R * R // T + DP * k : R * R // T + DP * (k + 1), :] = slab(9 + k).astype(BF)


def update_kernel(
    mine, sent, other, magnitude, nest_r, nest_l, fresh_r, fresh_l, new_r, new_l, out_r, out_l,
    halves, early, gram, step, mix, fac, tmp, fac_r, value_r, value_l, sems,
):
    copies = []

    def write(source, target):
        copies.append(pltpu.make_async_copy(source, target, sems.at[len(copies)]))
        copies[-1].start()

    write(fresh_r, new_r)
    write(fresh_l, new_l)

    first = lax.axis_index("core") == 1
    halves[...] = jnp.where(first, other[: DP * PIECE, :], mine[...]).astype(F32)
    base = R * R // T
    early[...] = jnp.where(first, sent[base:, :], other[base:, :]).astype(F32)
    slab, tile, put, both, unfold = unpacker(halves, early)
    gram[L:, :] = jnp.zeros((LP - L, LP), BF)
    gram[512:L, 512:] = jnp.where(iota((64, T), 1) < 64, slab(9), 0.0).astype(BF)
    both(gram, 0, 1, 5)
    both(gram, 0, 2, 6)
    both(gram, 0, 3, 7)
    both(gram, 1, 2, 8)
    both(gram, 1, 3, 9)
    both(gram, 2, 3, 10)
    unfold(gram, 0, 1, 11, 1)
    unfold(gram, 2, 3, 12, 2)
    for j in range(4):
        strip = jnp.concatenate([slab(26 + j), jnp.zeros((64, T), F32)], axis=0)
        gram[512:L, T * j : T * (j + 1)] = strip[:64].astype(BF)
        put(gram, j, 4, strip.T)
    for ref in (step, mix, fac, tmp):
        ref[L:, :] = jnp.zeros((LP - L, LP), BF)

    root = math.sqrt(D)
    contract = (((1,), (1,)), ((), ()))

    def apply(nest, magnitude, factor, rows, width, value, out):
        scaled = (nest[...] / magnitude).astype(BF)
        if width > rows:
            scaled = jnp.concatenate([scaled, jnp.zeros((ROWS, width - rows), BF)], axis=1)
        for start in range(0, rows, 256):
            stop = min(start + 256, rows)
            part = lax.dot_general(
                scaled, factor[start:stop, :], contract, preferred_element_type=F32
            )
            value[:, start:stop] = part * root
            write(value.at[:, start:stop], out.at[:, start:stop])

    for j in range(R // T):
        rows = slice(R * j, R * (j + 1))
        fac_r[:, T * j : T * (j + 1)] = jnp.where(first, sent[rows, :], other[rows, :])
    apply(nest_r, magnitude[0:1, 0:1], fac_r, R, R, value_r, out_r)
    factor = chain(gram, step, mix, fac, tmp, L, LP, True)
    apply(nest_l, magnitude[1:2, 0:1], factor, L, LP, value_l, out_l)
    for copy in copies:
        copy.wait()


def call(kernel, out_shape, scratch, name, *args):
    return pl.pallas_call(
        kernel,
        out_shape=out_shape,
        in_specs=[VMEM] * len(args),
        out_specs=jax.tree.map(lambda _: VMEM, out_shape),
        scratch_shapes=scratch,
        compiler_params=PARAMS,
        name=name,
    )(*args)


def router_call(mine):
    return call(
        router_kernel,
        jax.ShapeDtypeStruct((R * R // T + DP * 6, T), BF),
        [pltpu.VMEM((DP * PIECE, T), F32)] + [pltpu.VMEM((R, R), BF)] * 5,
        "router_chain", mine,
    )


def chain_call(mine, sent, other, magnitude, nest_r, nest_l, fresh_r, fresh_l):
    shape = jax.ShapeDtypeStruct
    return pl.pallas_call(
        update_kernel,
        out_shape=(shape((ROWS, R), F32), shape((ROWS, L), F32)) * 2,
        in_specs=[VMEM] * 8,
        out_specs=[pl.BlockSpec(memory_space=pl.ANY)] * 4,
        scratch_shapes=[pltpu.VMEM((DP * PIECE, T), F32), pltpu.VMEM((DP * 6, T), F32)]
        + [pltpu.VMEM((LP, LP), BF)] * 5
        + [pltpu.VMEM((R, R), BF), pltpu.VMEM((ROWS, R), F32), pltpu.VMEM((ROWS, L), F32)]
        + [pltpu.SemaphoreType.DMA((7,))],
        compiler_params=PARAMS,
        name="chain_apply",
    )(mine, sent, other, magnitude, nest_r, nest_l, fresh_r, fresh_l)


def local(router_grads, latent_grads, router_moment, latent_moment):
    shape = jax.ShapeDtypeStruct
    swap = [(0, 1), (1, 0)]
    grads = lax.optimization_barrier(jnp.concatenate([router_grads[0], latent_grads[0]], axis=1))
    other = lax.ppermute(grads, "core", swap)
    chip = call(chip_sum_kernel, shape((ROWS, R + L), BF), [], "chip_sum", grads, other)
    parts = lax.all_gather(chip, "x")
    fresh_r, fresh_l, nest_r, nest_l, payload = call(
        gram_kernel,
        (
            shape((ROWS, R), F32), shape((ROWS, L), F32),
            shape((ROWS, R), F32), shape((ROWS, L), F32),
            shape((DP * PIECE, T), BF),
        ),
        [pltpu.VMEM((DP * PIECE, T), F32)], "momentum_gram", parts, router_moment, latent_moment,
    )
    pieces = lax.all_to_all(payload.reshape(DP, PIECE, T), "dp", 0, 0)
    low, magnitude = call(
        scale_kernel,
        (shape((DP * PIECE, T), BF), shape((8, T), F32)),
        [], "scale_gram", pieces.reshape(DP * PIECE, T),
    )
    mine = lax.all_to_all(low.reshape(DP, PIECE, T), "dp", 0, 0).reshape(DP * PIECE, T)
    sent = router_call(mine)
    other = lax.ppermute(sent, "core", swap)
    return chain_call(mine, sent, other, magnitude, nest_r, nest_l, fresh_r, fresh_l)


def solution(mesh):
    inner = Mesh(mesh.devices.reshape(DP, 4, 2), ("dp", "x", "core"))
    group = ("x", "core")
    return jax.shard_map(
        local,
        mesh=inner,
        in_specs=(P(group, "dp", None), P(group, "dp", None), P("dp", None), P("dp", None)),
        out_specs=(P("dp", None),) * 4,
        check_vma=False,
    )
```

```python
import functools
import math

import jax
import jax.numpy as jnp
from jax import lax
from jax.experimental import pallas as pl
from jax.experimental.pallas import tpu as pltpu
from jax.sharding import Mesh
from jax.sharding import PartitionSpec as P

D = 7168
ITERS = 3
ROWS = 112
R = 384
L = 576
LP = 640
T = 128
DP = 64
SLABS = 15
PIECE = 16

COEF_A = 3.4445
COEF_B = -4.775
COEF_C = 2.0315
BETA = 0.95
EPSILON = 1e-07
BF = jnp.bfloat16
F32 = jnp.float32

VMEM = pl.BlockSpec(memory_space=pltpu.VMEM)
PARAMS = pltpu.CompilerParams(vmem_limit_bytes=48 * 1024 * 1024)


def dot(left, right):
    return jnp.dot(left, right, preferred_element_type=F32)


def iota(shape, dim):
    return lax.broadcasted_iota(jnp.int32, shape, dim)


def chip_sum_kernel(two, out):
    out[...] = (two[0] + two[1]).astype(BF)


def split3(value):
    high = value.astype(BF).astype(F32)
    rest = value - high
    middle = rest.astype(BF).astype(F32)
    return high, middle, rest - middle


def gram_kernel(parts, moment_r, moment_l, fresh_r, fresh_l, nest_r, nest_l, payload, slabs):
    core = lax.axis_index("core")
    squares = []
    grams = []
    for first, width, moment, new, nest in (
        (0, R, moment_r, fresh_r, nest_r),
        (R, L, moment_l, fresh_l, nest_l),
    ):
        part = [parts[k, :, first : first + width].astype(F32) for k in range(4)]
        summed = (part[0] + part[1]) + (part[2] + part[3])
        fresh = BETA * moment[...] + summed
        nesterov = summed + BETA * fresh
        new[...] = fresh
        nest[...] = nesterov
        squares.append(jnp.sum(nesterov * nesterov))
        low = nesterov.astype(BF)
        if width == L:
            low = jnp.concatenate([low, jnp.zeros((ROWS, LP - L), BF)], axis=1)
        gram = lax.dot_general(low, low, (((0,), (0,)), ((), ())), preferred_element_type=F32)
        grams.append(gram)

    def tile(k, i, j):
        return grams[k][T * i : T * (i + 1), T * j : T * (j + 1)]

    row, lane = iota((T, T), 0), iota((T, T), 1)

    def fold(upper, lower):
        return jnp.where(row <= lane, upper, lower)

    half = iota((64, T), 1) < 64
    last = tile(0, 2, 2)
    corner = jnp.where(half, tile(1, 4, 4)[:64], last[64:])
    tiles = [
        tile(0, 0, 1),
        tile(0, 0, 2),
        tile(0, 1, 2),
        fold(tile(0, 0, 0), tile(0, 1, 1)),
        jnp.concatenate([last[:64], corner], axis=0),
        tile(1, 0, 1),
        tile(1, 0, 2),
        tile(1, 0, 3),
        tile(1, 1, 2),
        tile(1, 1, 3),
        tile(1, 2, 3),
        fold(tile(1, 0, 0), tile(1, 1, 1)),
        fold(tile(1, 2, 2), tile(1, 3, 3)),
    ]
    pieces = [t[64 * h : 64 * (h + 1)] for t in tiles for h in range(2)]
    pieces += [grams[1][512:576, T * j : T * (j + 1)] for j in range(4)]

    parts6 = split3(squares[0]) + split3(squares[1])
    lane1 = iota((64, T), 1)
    row1 = iota((64, T), 0)
    extra = jnp.zeros((64, T), F32)
    for k in range(6):
        extra = jnp.where(lane1 == k, parts6[k], extra)
    for k, (which, i) in enumerate(((0, 1), (1, 1), (1, 3))):
        diagonal = jnp.sum(jnp.where(row == lane, tile(which, i, i), 0.0), axis=0, keepdims=True)
        low_half = pltpu.roll(diagonal, 64, 1)
        extra = jnp.where((row1 == 2 * k) & (lane1 >= 64), low_half, extra)
        extra = jnp.where((row1 == 2 * k + 1) & (lane1 >= 64), diagonal, extra)

    for c in range(2):

        @pl.when(core == c)
        def _():
            for s in range(SLABS):
                slabs[pl.ds(s, DP, stride=PIECE), :] = pieces[SLABS * (1 - c) + s]

    slabs[pl.ds(SLABS, DP, stride=PIECE), :] = extra
    payload[...] = slabs[...].astype(BF)


def scale_kernel(pieces, low, magnitude):
    core, here = lax.axis_index("core"), lax.axis_index("dp")
    total = jnp.sum(pieces[...].reshape(DP, PIECE, T).astype(F32), axis=0)
    last = total[SLABS : SLABS + 1]
    lane1 = iota((1, T), 1)
    router = jnp.sum(jnp.where(lane1 < 3, last, 0.0), axis=1, keepdims=True)
    latent = jnp.sum(jnp.where((lane1 >= 3) & (lane1 < 6), last, 0.0), axis=1, keepdims=True)
    router = jnp.sqrt(router) + EPSILON
    latent = jnp.sqrt(latent) + EPSILON
    inverse_r = 1.0 / (router * router)
    inverse_l = 1.0 / (latent * latent)
    row, lane = iota((PIECE, T), 0), iota((PIECE, T), 1)
    slab = SLABS * (1 - core) + row
    of_router = (slab < 9) | ((slab == 9) & (lane >= 64))
    of_router = jnp.where(row == SLABS, jnp.where(here < 2, 1, 0), jnp.where(of_router, 1, 0))
    scaled = (total * jnp.where(of_router == 1, inverse_r, inverse_l)).astype(BF)
    for k in range(DP):
        low[PIECE * k : PIECE * (k + 1), :] = scaled
    magnitude[...] = jnp.where(iota((8, T), 0) == 0, router, latent)


def unpacker(half, early=None):
    row, lane = iota((T, T), 0), iota((T, T), 1)
    lane1 = iota((1, T), 1)
    extra = half[pl.ds(SLABS, 8, stride=PIECE), :]

    def slab(g):
        if early is None:
            return half[pl.ds(g, DP, stride=PIECE), :]
        if g < SLABS:
            return early[DP * (g - 9) : DP * (g - 8), :]
        return half[pl.ds(g - SLABS, DP, stride=PIECE), :]

    def tile(t):
        return jnp.concatenate([slab(2 * t), slab(2 * t + 1)], axis=0)

    def put(ref, i, j, value):
        ref[T * i : T * (i + 1), T * j : T * (j + 1)] = value.astype(BF)

    def both(ref, i, j, t):
        value = tile(t)
        put(ref, i, j, value)
        put(ref, j, i, value.T)

    def unfold(ref, i, j, t, k):
        value = tile(t)
        flipped = value.T
        put(ref, i, i, jnp.where(row <= lane, value, flipped))
        low_half = pltpu.roll(extra[2 * k : 2 * k + 1], 64, 1)
        diagonal = jnp.where(lane1 < 64, low_half, extra[2 * k + 1 : 2 * k + 2])
        inner = jnp.where(row > lane, value, flipped)
        put(ref, j, j, jnp.where(row == lane, diagonal, inner))

    return slab, tile, put, both, unfold


def strips(left, right, rows, width, epilogue, symmetric=False):
    edge = (rows - 1) // 256 * 256 if symmetric else width
    for start in range(0, edge, 256):
        stop = min(start + 256, edge)
        acc = dot(left[:rows, :], right[:, start:stop])
        for ref, value in epilogue(acc, 0, start, stop):
            ref[:rows, start:stop] = value
            if symmetric:
                strip = value[edge:rows].astype(F32)
                if rows - edge < T:
                    strip = jnp.concatenate([strip, jnp.zeros((T + edge - rows, 256), F32)], axis=0)
                ref[start:stop, edge:width] = strip.T.astype(BF)
    if symmetric:
        acc = dot(left[edge:rows, :], right[:, edge:width])
        for ref, value in epilogue(acc, edge, edge, width):
            ref[edge:rows, edge:width] = value


def product(left, right, rows, width, epilogue, symmetric=0):
    for start in range(0, width, 256):
        stop = min(start + 256, width)
        top = start if symmetric else 0
        acc = dot(left[top:rows, :], right[:, start:stop])
        for ref, value in epilogue(acc, top, start, stop):
            ref[top:rows, start:stop] = value
            if symmetric and stop < width:
                below = value[stop - top :].astype(F32)
                if rows < width:
                    below = jnp.concatenate([below, jnp.zeros((width - rows, 256), F32)], axis=0)
                ref[start:stop, stop:width] = below.T.astype(BF)


def chain(gram, step, mix, fac, tmp, rows, width, symmetric):
    def store(ref):
        return lambda acc, top, start, stop: [(ref, acc.astype(BF))]

    def mixture(now, acc, top, start, stop):
        squared = acc.astype(BF).astype(F32)
        value = COEF_B * now[top : top + acc.shape[0], start:stop].astype(F32) + COEF_C * squared
        return value.astype(BF)

    def begin(acc, top, start, stop):
        value = mixture(gram, acc, top, start, stop)
        eye = (iota(acc.shape, 0) + top == iota(acc.shape, 1) + start).astype(F32)
        return [(fac, (COEF_A * eye + value.astype(F32)).astype(BF))]

    product(gram, gram, rows, width, begin, True)
    for iteration in range(1, ITERS):

        def mixing(acc, top, start, stop):
            return [(mix, mixture(step, acc, top, start, stop))]

        def blend(acc, top, start, stop, fac=fac, tmp=tmp):
            value = COEF_A * fac[top : top + acc.shape[0], start:stop].astype(F32) + acc
            return [(tmp, value.astype(BF))]

        strips(fac, gram, rows, width, store(tmp), symmetric and iteration == 1)
        strips(tmp, fac, rows, width, store(step), symmetric)
        strips(step, step, rows, width, mixing, symmetric)
        strips(mix, fac, rows, width, blend, symmetric)
        fac, tmp = tmp, fac
    return fac


def router_kernel(mine, out, half, gram, step, mix, fac, tmp):
    @pl.when(lax.axis_index("core") == 0)
    def _():
        out[: DP * PIECE, :] = mine[...]

    @pl.when(lax.axis_index("core") == 1)
    def _():
        half[...] = mine[...].astype(F32)
        slab, tile, put, both, unfold = unpacker(half)
        both(gram, 0, 1, 0)
        both(gram, 0, 2, 1)
        both(gram, 1, 2, 2)
        unfold(gram, 0, 1, 3, 0)
        last = tile(4)
        upper = iota((T, T), 0) <= iota((T, T), 1)
        put(gram, 2, 2, jnp.where(upper, last, last.T))
        factor = chain(gram, step, mix, fac, tmp, R, R, False)
        for j in range(R // T):
            out[R * j : R * (j + 1), :] = factor[:, T * j : T * (j + 1)]
        for k in range(6):
            out[R * R // T + DP * k : R * R // T + DP * (k + 1), :] = slab(9 + k).astype(BF)


def update_kernel(
    two, magnitude, nest_r, nest_l, fresh_r, fresh_l, new_r, new_l, out_r, out_l,
    halves, early, gram, step, mix, fac, tmp, fac_r, value_r, value_l, sems,
):
    copies = []

    def write(source, target):
        copies.append(pltpu.make_async_copy(source, target, sems.at[len(copies)]))
        copies[-1].start()

    write(fresh_r, new_r)
    write(fresh_l, new_l)

    halves[...] = two[0, : DP * PIECE, :].astype(F32)
    early[...] = two[1, R * R // T :, :].astype(F32)
    slab, tile, put, both, unfold = unpacker(halves, early)
    gram[L:, :] = jnp.zeros((LP - L, LP), BF)
    gram[512:L, 512:] = jnp.where(iota((64, T), 1) < 64, slab(9), 0.0).astype(BF)
    both(gram, 0, 1, 5)
    both(gram, 0, 2, 6)
    both(gram, 0, 3, 7)
    both(gram, 1, 2, 8)
    both(gram, 1, 3, 9)
    both(gram, 2, 3, 10)
    unfold(gram, 0, 1, 11, 1)
    unfold(gram, 2, 3, 12, 2)
    for j in range(4):
        strip = jnp.concatenate([slab(26 + j), jnp.zeros((64, T), F32)], axis=0)
        gram[512:L, T * j : T * (j + 1)] = strip[:64].astype(BF)
        put(gram, j, 4, strip.T)
    for ref in (step, mix, fac, tmp):
        ref[L:, :] = jnp.zeros((LP - L, LP), BF)

    root = math.sqrt(D)
    contract = (((1,), (1,)), ((), ()))

    def apply(nest, magnitude, factor, rows, width, value, out):
        scaled = (nest[...] / magnitude).astype(BF)
        if width > rows:
            scaled = jnp.concatenate([scaled, jnp.zeros((ROWS, width - rows), BF)], axis=1)
        for start in range(0, rows, 256):
            stop = min(start + 256, rows)
            part = lax.dot_general(
                scaled, factor[start:stop, :], contract, preferred_element_type=F32
            )
            value[:, start:stop] = part * root
            write(value.at[:, start:stop], out.at[:, start:stop])

    for j in range(R // T):
        rows = slice(R * j, R * (j + 1))
        fac_r[:, T * j : T * (j + 1)] = two[1, rows, :]
    apply(nest_r, magnitude[0:1, 0:1], fac_r, R, R, value_r, out_r)
    factor = chain(gram, step, mix, fac, tmp, L, LP, True)
    apply(nest_l, magnitude[1:2, 0:1], factor, L, LP, value_l, out_l)
    for copy in copies:
        copy.wait()


def call(kernel, out_shape, scratch, name, *args):
    return pl.pallas_call(
        kernel,
        out_shape=out_shape,
        in_specs=[VMEM] * len(args),
        out_specs=jax.tree.map(lambda _: VMEM, out_shape),
        scratch_shapes=scratch,
        compiler_params=PARAMS,
        name=name,
    )(*args)


def router_call(mine):
    return call(
        router_kernel,
        jax.ShapeDtypeStruct((R * R // T + DP * 6, T), BF),
        [pltpu.VMEM((DP * PIECE, T), F32)] + [pltpu.VMEM((R, R), BF)] * 5,
        "router_chain", mine,
    )


def chain_call(two, magnitude, nest_r, nest_l, fresh_r, fresh_l):
    shape = jax.ShapeDtypeStruct
    return pl.pallas_call(
        update_kernel,
        out_shape=(shape((ROWS, R), F32), shape((ROWS, L), F32)) * 2,
        in_specs=[VMEM] * 6,
        out_specs=[pl.BlockSpec(memory_space=pl.ANY)] * 4,
        scratch_shapes=[pltpu.VMEM((DP * PIECE, T), F32), pltpu.VMEM((DP * 6, T), F32)]
        + [pltpu.VMEM((LP, LP), BF)] * 5
        + [pltpu.VMEM((R, R), BF), pltpu.VMEM((ROWS, R), F32), pltpu.VMEM((ROWS, L), F32)]
        + [pltpu.SemaphoreType.DMA((7,))],
        compiler_params=PARAMS,
        name="chain_apply",
    )(two, magnitude, nest_r, nest_l, fresh_r, fresh_l)


def local(router_grads, latent_grads, router_moment, latent_moment):
    shape = jax.ShapeDtypeStruct
    grads = lax.optimization_barrier(jnp.concatenate([router_grads[0], latent_grads[0]], axis=1))
    two = lax.all_gather(grads, "core")
    chip = call(chip_sum_kernel, shape((ROWS, R + L), BF), [], "chip_sum", two)
    parts = lax.all_gather(chip, "x")
    fresh_r, fresh_l, nest_r, nest_l, payload = call(
        gram_kernel,
        (
            shape((ROWS, R), F32), shape((ROWS, L), F32),
            shape((ROWS, R), F32), shape((ROWS, L), F32),
            shape((DP * PIECE, T), BF),
        ),
        [pltpu.VMEM((DP * PIECE, T), F32)], "momentum_gram", parts, router_moment, latent_moment,
    )
    pieces = lax.all_to_all(payload.reshape(DP, PIECE, T), "dp", 0, 0)
    low, magnitude = call(
        scale_kernel,
        (shape((DP * PIECE, T), BF), shape((8, T), F32)),
        [], "scale_gram", pieces.reshape(DP * PIECE, T),
    )
    mine = lax.all_to_all(low.reshape(DP, PIECE, T), "dp", 0, 0).reshape(DP * PIECE, T)
    sent = router_call(mine)
    two = lax.all_gather(sent, "core")
    return chain_call(two, magnitude, nest_r, nest_l, fresh_r, fresh_l)


def solution(mesh):
    inner = Mesh(mesh.devices.reshape(DP, 4, 2), ("dp", "x", "core"))
    group = ("x", "core")
    return jax.shard_map(
        local,
        mesh=inner,
        in_specs=(P(group, "dp", None), P(group, "dp", None), P("dp", None), P("dp", None)),
        out_specs=(P("dp", None),) * 4,
        check_vma=False,
    )
```

```python
import functools
import math

import jax
import jax.numpy as jnp
from jax import lax
from jax.experimental import pallas as pl
from jax.experimental.pallas import tpu as pltpu
from jax.sharding import Mesh
from jax.sharding import PartitionSpec as P

D = 7168
ITERS = 3
ROWS = 112
R = 384
L = 576
LP = 640
T = 128
DP = 64
SLABS = 15
XROWS = ROWS * (R + L) // T
PIECE = 16

COEF_A = 3.4445
COEF_B = -4.775
COEF_C = 2.0315
BETA = 0.95
EPSILON = 1e-07
BF = jnp.bfloat16
F32 = jnp.float32

VMEM = pl.BlockSpec(memory_space=pltpu.VMEM)
PARAMS = pltpu.CompilerParams(vmem_limit_bytes=48 * 1024 * 1024)


def dot(left, right):
    return jnp.dot(left, right, preferred_element_type=F32)


def iota(shape, dim):
    return lax.broadcasted_iota(jnp.int32, shape, dim)


def chip_sum_kernel(two, out):
    for j in range(7):
        total = two[0, :, T * j : T * (j + 1)] + two[1, :, T * j : T * (j + 1)]
        out[ROWS * j : ROWS * (j + 1), :] = total.astype(BF)
    last = two[0, :, 7 * T :] + two[1, :, 7 * T :]
    out[7 * ROWS :, :] = jnp.concatenate([last[: ROWS // 2], last[ROWS // 2 :]], axis=1).astype(BF)


def split3(value):
    high = value.astype(BF).astype(F32)
    rest = value - high
    middle = rest.astype(BF).astype(F32)
    return high, middle, rest - middle


def gram_kernel(parts, moment_r, moment_l, fresh_r, fresh_l, nest_r, nest_l, payload, slabs):
    core = lax.axis_index("core")
    part = [parts[k].astype(F32) for k in range(4)]
    total = (part[0] + part[1]) + (part[2] + part[3])
    last = total[7 * ROWS :]
    last = jnp.concatenate([last[:, :64], last[:, 64:]], axis=0)
    total = [total[ROWS * j : ROWS * (j + 1)] for j in range(7)]
    total = jnp.concatenate(total + [last], axis=1)
    squares = []
    grams = []
    for first, width, moment, new, nest in (
        (0, R, moment_r, fresh_r, nest_r),
        (R, L, moment_l, fresh_l, nest_l),
    ):
        summed = total[:, first : first + width]
        fresh = BETA * moment[...] + summed
        nesterov = summed + BETA * fresh
        new[...] = fresh
        nest[...] = nesterov
        squares.append(jnp.sum(nesterov * nesterov))
        low = nesterov.astype(BF)
        if width == L:
            low = jnp.concatenate([low, jnp.zeros((ROWS, LP - L), BF)], axis=1)
        gram = lax.dot_general(low, low, (((0,), (0,)), ((), ())), preferred_element_type=F32)
        grams.append(gram)

    def tile(k, i, j):
        return grams[k][T * i : T * (i + 1), T * j : T * (j + 1)]

    row, lane = iota((T, T), 0), iota((T, T), 1)

    def fold(upper, lower):
        return jnp.where(row <= lane, upper, lower)

    half = iota((64, T), 1) < 64
    last = tile(0, 2, 2)
    corner = jnp.where(half, tile(1, 4, 4)[:64], last[64:])
    tiles = [
        tile(0, 0, 1),
        tile(0, 0, 2),
        tile(0, 1, 2),
        fold(tile(0, 0, 0), tile(0, 1, 1)),
        jnp.concatenate([last[:64], corner], axis=0),
        tile(1, 0, 1),
        tile(1, 0, 2),
        tile(1, 0, 3),
        tile(1, 1, 2),
        tile(1, 1, 3),
        tile(1, 2, 3),
        fold(tile(1, 0, 0), tile(1, 1, 1)),
        fold(tile(1, 2, 2), tile(1, 3, 3)),
    ]
    pieces = [t[64 * h : 64 * (h + 1)] for t in tiles for h in range(2)]
    pieces += [grams[1][512:576, T * j : T * (j + 1)] for j in range(4)]

    parts6 = split3(squares[0]) + split3(squares[1])
    lane1 = iota((64, T), 1)
    row1 = iota((64, T), 0)
    extra = jnp.zeros((64, T), F32)
    for k in range(6):
        extra = jnp.where(lane1 == k, parts6[k], extra)
    for k, (which, i) in enumerate(((0, 1), (1, 1), (1, 3))):
        diagonal = jnp.sum(jnp.where(row == lane, tile(which, i, i), 0.0), axis=0, keepdims=True)
        low_half = pltpu.roll(diagonal, 64, 1)
        extra = jnp.where((row1 == 2 * k) & (lane1 >= 64), low_half, extra)
        extra = jnp.where((row1 == 2 * k + 1) & (lane1 >= 64), diagonal, extra)

    for c in range(2):

        @pl.when(core == c)
        def _():
            for s in range(SLABS):
                slabs[pl.ds(s, DP, stride=PIECE), :] = pieces[SLABS * (1 - c) + s]

    slabs[pl.ds(SLABS, DP, stride=PIECE), :] = extra
    payload[...] = slabs[...].astype(BF)


def scale_kernel(pieces, low, magnitude):
    core, here = lax.axis_index("core"), lax.axis_index("dp")
    total = jnp.sum(pieces[...].reshape(DP, PIECE, T).astype(F32), axis=0)
    last = total[SLABS : SLABS + 1]
    lane1 = iota((1, T), 1)
    router = jnp.sum(jnp.where(lane1 < 3, last, 0.0), axis=1, keepdims=True)
    latent = jnp.sum(jnp.where((lane1 >= 3) & (lane1 < 6), last, 0.0), axis=1, keepdims=True)
    router = jnp.sqrt(router) + EPSILON
    latent = jnp.sqrt(latent) + EPSILON
    inverse_r = 1.0 / (router * router)
    inverse_l = 1.0 / (latent * latent)
    row, lane = iota((PIECE, T), 0), iota((PIECE, T), 1)
    slab = SLABS * (1 - core) + row
    of_router = (slab < 9) | ((slab == 9) & (lane >= 64))
    of_router = jnp.where(row == SLABS, jnp.where(here < 2, 1, 0), jnp.where(of_router, 1, 0))
    scaled = (total * jnp.where(of_router == 1, inverse_r, inverse_l)).astype(BF)
    for k in range(DP):
        low[PIECE * k : PIECE * (k + 1), :] = scaled
    magnitude[...] = jnp.where(iota((8, T), 0) == 0, router, latent)


def unpacker(half, early=None):
    row, lane = iota((T, T), 0), iota((T, T), 1)
    lane1 = iota((1, T), 1)
    extra = half[pl.ds(SLABS, 8, stride=PIECE), :]

    def slab(g):
        if early is None:
            return half[pl.ds(g, DP, stride=PIECE), :]
        if g < SLABS:
            return early[DP * (g - 9) : DP * (g - 8), :]
        return half[pl.ds(g - SLABS, DP, stride=PIECE), :]

    def tile(t):
        return jnp.concatenate([slab(2 * t), slab(2 * t + 1)], axis=0)

    def put(ref, i, j, value):
        ref[T * i : T * (i + 1), T * j : T * (j + 1)] = value.astype(BF)

    def both(ref, i, j, t):
        value = tile(t)
        put(ref, i, j, value)
        put(ref, j, i, value.T)

    def unfold(ref, i, j, t, k):
        value = tile(t)
        flipped = value.T
        put(ref, i, i, jnp.where(row <= lane, value, flipped))
        low_half = pltpu.roll(extra[2 * k : 2 * k + 1], 64, 1)
        diagonal = jnp.where(lane1 < 64, low_half, extra[2 * k + 1 : 2 * k + 2])
        inner = jnp.where(row > lane, value, flipped)
        put(ref, j, j, jnp.where(row == lane, diagonal, inner))

    return slab, tile, put, both, unfold


def strips(left, right, rows, width, epilogue, symmetric=False):
    edge = (rows - 1) // 256 * 256 if symmetric else width
    for start in range(0, edge, 256):
        stop = min(start + 256, edge)
        acc = dot(left[:rows, :], right[:, start:stop])
        for ref, value in epilogue(acc, 0, start, stop):
            ref[:rows, start:stop] = value
            if symmetric:
                strip = value[edge:rows].astype(F32)
                if rows - edge < T:
                    strip = jnp.concatenate([strip, jnp.zeros((T + edge - rows, 256), F32)], axis=0)
                ref[start:stop, edge:width] = strip.T.astype(BF)
    if symmetric:
        acc = dot(left[edge:rows, :], right[:, edge:width])
        for ref, value in epilogue(acc, edge, edge, width):
            ref[edge:rows, edge:width] = value


def product(left, right, rows, width, epilogue, symmetric=0):
    for start in range(0, width, 256):
        stop = min(start + 256, width)
        top = start if symmetric else 0
        acc = dot(left[top:rows, :], right[:, start:stop])
        for ref, value in epilogue(acc, top, start, stop):
            ref[top:rows, start:stop] = value
            if symmetric and stop < width:
                below = value[stop - top :].astype(F32)
                if rows < width:
                    below = jnp.concatenate([below, jnp.zeros((width - rows, 256), F32)], axis=0)
                ref[start:stop, stop:width] = below.T.astype(BF)


def chain(gram, step, mix, fac, tmp, rows, width, symmetric):
    def store(ref):
        return lambda acc, top, start, stop: [(ref, acc.astype(BF))]

    def mixture(now, acc, top, start, stop):
        squared = acc.astype(BF).astype(F32)
        value = COEF_B * now[top : top + acc.shape[0], start:stop].astype(F32) + COEF_C * squared
        return value.astype(BF)

    def begin(acc, top, start, stop):
        value = mixture(gram, acc, top, start, stop)
        eye = (iota(acc.shape, 0) + top == iota(acc.shape, 1) + start).astype(F32)
        return [(fac, (COEF_A * eye + value.astype(F32)).astype(BF))]

    product(gram, gram, rows, width, begin, True)
    for iteration in range(1, ITERS):

        def mixing(acc, top, start, stop):
            return [(mix, mixture(step, acc, top, start, stop))]

        def blend(acc, top, start, stop, fac=fac, tmp=tmp):
            value = COEF_A * fac[top : top + acc.shape[0], start:stop].astype(F32) + acc
            return [(tmp, value.astype(BF))]

        strips(fac, gram, rows, width, store(tmp), symmetric and iteration == 1)
        strips(tmp, fac, rows, width, store(step), symmetric)
        strips(step, step, rows, width, mixing, symmetric)
        strips(mix, fac, rows, width, blend, symmetric)
        fac, tmp = tmp, fac
    return fac


def router_kernel(mine, out, half, gram, step, mix, fac, tmp):
    @pl.when(lax.axis_index("core") == 0)
    def _():
        out[: DP * PIECE, :] = mine[...]

    @pl.when(lax.axis_index("core") == 1)
    def _():
        half[...] = mine[...].astype(F32)
        slab, tile, put, both, unfold = unpacker(half)
        both(gram, 0, 1, 0)
        both(gram, 0, 2, 1)
        both(gram, 1, 2, 2)
        unfold(gram, 0, 1, 3, 0)
        last = tile(4)
        upper = iota((T, T), 0) <= iota((T, T), 1)
        put(gram, 2, 2, jnp.where(upper, last, last.T))
        factor = chain(gram, step, mix, fac, tmp, R, R, False)
        for j in range(R // T):
            out[R * j : R * (j + 1), :] = factor[:, T * j : T * (j + 1)]
        for k in range(6):
            out[R * R // T + DP * k : R * R // T + DP * (k + 1), :] = slab(9 + k).astype(BF)


def update_kernel(
    two, magnitude, nest_r, nest_l, fresh_r, fresh_l, new_r, new_l, out_r, out_l,
    halves, early, gram, step, mix, fac, tmp, fac_r, value_r, value_l, sems,
):
    copies = []

    def write(source, target):
        copies.append(pltpu.make_async_copy(source, target, sems.at[len(copies)]))
        copies[-1].start()

    write(fresh_r, new_r)
    write(fresh_l, new_l)

    halves[...] = two[0, : DP * PIECE, :].astype(F32)
    early[...] = two[1, R * R // T :, :].astype(F32)
    slab, tile, put, both, unfold = unpacker(halves, early)
    gram[L:, :] = jnp.zeros((LP - L, LP), BF)
    gram[512:L, 512:] = jnp.where(iota((64, T), 1) < 64, slab(9), 0.0).astype(BF)
    both(gram, 0, 1, 5)
    both(gram, 0, 2, 6)
    both(gram, 0, 3, 7)
    both(gram, 1, 2, 8)
    both(gram, 1, 3, 9)
    both(gram, 2, 3, 10)
    unfold(gram, 0, 1, 11, 1)
    unfold(gram, 2, 3, 12, 2)
    for j in range(4):
        strip = jnp.concatenate([slab(26 + j), jnp.zeros((64, T), F32)], axis=0)
        gram[512:L, T * j : T * (j + 1)] = strip[:64].astype(BF)
        put(gram, j, 4, strip.T)
    for ref in (step, mix, fac, tmp):
        ref[L:, :] = jnp.zeros((LP - L, LP), BF)

    root = math.sqrt(D)
    contract = (((1,), (1,)), ((), ()))

    def apply(nest, magnitude, factor, rows, width, value, out):
        scaled = (nest[...] / magnitude).astype(BF)
        if width > rows:
            scaled = jnp.concatenate([scaled, jnp.zeros((ROWS, width - rows), BF)], axis=1)
        for start in range(0, rows, 256):
            stop = min(start + 256, rows)
            part = lax.dot_general(
                scaled, factor[start:stop, :], contract, preferred_element_type=F32
            )
            value[:, start:stop] = part * root
            write(value.at[:, start:stop], out.at[:, start:stop])

    for j in range(R // T):
        rows = slice(R * j, R * (j + 1))
        fac_r[:, T * j : T * (j + 1)] = two[1, rows, :]
    apply(nest_r, magnitude[0:1, 0:1], fac_r, R, R, value_r, out_r)
    factor = chain(gram, step, mix, fac, tmp, L, LP, True)
    apply(nest_l, magnitude[1:2, 0:1], factor, L, LP, value_l, out_l)
    for copy in copies:
        copy.wait()


def call(kernel, out_shape, scratch, name, *args):
    return pl.pallas_call(
        kernel,
        out_shape=out_shape,
        in_specs=[VMEM] * len(args),
        out_specs=jax.tree.map(lambda _: VMEM, out_shape),
        scratch_shapes=scratch,
        compiler_params=PARAMS,
        name=name,
    )(*args)


def router_call(mine):
    return call(
        router_kernel,
        jax.ShapeDtypeStruct((R * R // T + DP * 6, T), BF),
        [pltpu.VMEM((DP * PIECE, T), F32)] + [pltpu.VMEM((R, R), BF)] * 5,
        "router_chain", mine,
    )


def chain_call(two, magnitude, nest_r, nest_l, fresh_r, fresh_l):
    shape = jax.ShapeDtypeStruct
    return pl.pallas_call(
        update_kernel,
        out_shape=(shape((ROWS, R), F32), shape((ROWS, L), F32)) * 2,
        in_specs=[VMEM] * 6,
        out_specs=[pl.BlockSpec(memory_space=pl.ANY)] * 4,
        scratch_shapes=[pltpu.VMEM((DP * PIECE, T), F32), pltpu.VMEM((DP * 6, T), F32)]
        + [pltpu.VMEM((LP, LP), BF)] * 5
        + [pltpu.VMEM((R, R), BF), pltpu.VMEM((ROWS, R), F32), pltpu.VMEM((ROWS, L), F32)]
        + [pltpu.SemaphoreType.DMA((7,))],
        compiler_params=PARAMS,
        name="chain_apply",
    )(two, magnitude, nest_r, nest_l, fresh_r, fresh_l)


def local(router_grads, latent_grads, router_moment, latent_moment):
    shape = jax.ShapeDtypeStruct
    grads = lax.optimization_barrier(jnp.concatenate([router_grads[0], latent_grads[0]], axis=1))
    two = lax.all_gather(grads, "core")
    chip = call(chip_sum_kernel, shape((XROWS, T), BF), [], "chip_sum", two)
    parts = lax.all_gather(chip, "x")
    fresh_r, fresh_l, nest_r, nest_l, payload = call(
        gram_kernel,
        (
            shape((ROWS, R), F32), shape((ROWS, L), F32),
            shape((ROWS, R), F32), shape((ROWS, L), F32),
            shape((DP * PIECE, T), BF),
        ),
        [pltpu.VMEM((DP * PIECE, T), F32)], "momentum_gram", parts, router_moment, latent_moment,
    )
    pieces = lax.all_to_all(payload.reshape(DP, PIECE, T), "dp", 0, 0)
    low, magnitude = call(
        scale_kernel,
        (shape((DP * PIECE, T), BF), shape((8, T), F32)),
        [], "scale_gram", pieces.reshape(DP * PIECE, T),
    )
    mine = lax.all_to_all(low.reshape(DP, PIECE, T), "dp", 0, 0).reshape(DP * PIECE, T)
    sent = router_call(mine)
    two = lax.all_gather(sent, "core")
    return chain_call(two, magnitude, nest_r, nest_l, fresh_r, fresh_l)


def solution(mesh):
    inner = Mesh(mesh.devices.reshape(DP, 4, 2), ("dp", "x", "core"))
    group = ("x", "core")
    return jax.shard_map(
        local,
        mesh=inner,
        in_specs=(P(group, "dp", None), P(group, "dp", None), P("dp", None), P("dp", None)),
        out_specs=(P("dp", None),) * 4,
        check_vma=False,
    )
```
